32 devices in a mesh: seq: 8 (over z, y), store: 4 (over x, core).
Axes of the slice: x: 2, y: 2, z: 4, core: 2. Of those that a mesh axis runs over, the one named last changes fastest.
Arguments:
- hidden: bfloat16 [8192, 4096], P('seq'), may hold values from -6 to 6
- nbr_table: bfloat16 [32, 128, 896], P('store'), may hold values from -6 to 6
- nbr_ids: int32 [128, 2], P('seq'), may hold values from 0 to 31, as said below
- w_query: bfloat16 [4096, 4096], P(None, 'store'), may hold values from -0.09375 to 0.09375
- w_key: bfloat16 [896, 4096], P(None, 'store'), may hold values from -0.1875 to 0.1875
- w_value: bfloat16 [896, 4096], P(None, 'store'), may hold values from -0.1875 to 0.1875
- w_out: bfloat16 [4096, 4096], P('store'), may hold values from -0.125 to 0.125
- enc_query: bfloat16 [896, 896], replicated, may hold values from -0.1875 to 0.1875
- enc_key: bfloat16 [4096, 896], P('seq'), may hold values from -0.09375 to 0.09375
- enc_value: bfloat16 [4096, 896], P('seq'), may hold values from -0.09375 to 0.09375
- enc_out: bfloat16 [896, 896], replicated, may hold values from -0.1875 to 0.1875
Outputs:
- cross_out: bfloat16 [8192, 4096], P('seq', 'store')
The draws below stay inside these ranges and needn't reach their ends.
Inputs may be any that keep to these rules, and one draw needn't show every extreme that they name: `nbr_ids`: among the spans of one index of seq (16 consecutive spans), the ids fall in each owner's range k * 8 to k * 8 + 7 exactly 8 times.
All inputs are finite; a program needn't handle non-finite values.
Results may differ from the reference program's by a relative error of at most 0.03.
Values may be sent and summed in bfloat16 or wider, within the bound.
A program may use at most 128 MiB of HBM per device.

```python
import math
import jax
import jax.numpy as jnp
from jax import lax

D = 4096
HEADS = 32
HD = 128
E = 896
EHEADS = 14
EHD = 64
CH = 64
NLEN = 128
KNB = 2
TOKENS = 8192
CPR = 16
SPANS = 128
ROW_REQ = 32
REQ = 8
BLK_DEV = 8
BLOCKS = 32
HG = 8
N_STORE = 4


def draw_nbr_ids(key, part):

    def one_shard(shard):
        shard_key = jax.random.fold_in(key, shard)
        order = jax.random.permutation(jax.random.fold_in(shard_key, 1), ROW_REQ)
        owners = order // REQ
        within = jax.random.randint(jax.random.fold_in(shard_key, 2), (ROW_REQ,), 0, BLK_DEV)
        within = jnp.where(order == 0, 0, jnp.where(order == ROW_REQ - 1, BLK_DEV - 1, within))
        return (owners * BLK_DEV + within).reshape(CPR, KNB)
    shards = jax.vmap(one_shard)(jnp.arange(SPANS // CPR, dtype=jnp.int32))
    return shards.reshape(SPANS, KNB).astype(jnp.int32)


def raised(array, own_key, source, target, parts, factor):
    owner, partner = [(jnp.arange(array.shape[axis_at]) // (array.shape[axis_at] // parts)).reshape([-1 if axis == axis_at else 1 for axis in range(array.ndim)]) for axis_at in (source, target)]
    chosen = jax.random.permutation(own_key, parts)[partner]
    strong = (owner == chosen) | (owner == (partner + parts // 2) % parts)
    return jnp.where(strong, factor * array, array)


def shard_levels(key, extent, split, least, largest):
    factor_of = 1.0
    for axis_at, blocks in split:
        draws = jax.random.uniform(jax.random.fold_in(jax.random.fold_in(key, 6), axis_at), (blocks,), jnp.float32, least / len(split), largest / len(split))
        factor_of = factor_of * jnp.repeat(jnp.exp(draws), extent[axis_at] // blocks).reshape((-1,) + (1,) * (len(extent) - 1 - axis_at))
    return factor_of


def centred(own_key, shape, width, limit, pieces=(), kind=jnp.bfloat16):
    result = jax.random.normal(own_key, shape, jnp.float32) * width
    if len(pieces) > 0:
        result = shard_levels(own_key, shape, pieces, -0.22, 0.18) * result
    return jnp.clip(result, min=-limit, max=limit).astype(kind)


def bell_draw_with(own_key, dims, width, most, cuts, heavy, kind=jnp.bfloat16):
    values = width * jax.random.normal(own_key, dims, jnp.float32)
    if cuts:
        values = values * shard_levels(own_key, dims, cuts, -0.22, 0.18)
    return jnp.clip(raised(values, jax.random.fold_in(own_key, 3), *heavy), -most, most).astype(kind)


def setup_inputs(seed: int = 0) -> dict:
    key_list = jax.random.split(jax.random.key(seed), 12)
    return {
        "hidden": centred(key_list[0], (TOKENS, D), 1.0, 6.0, ((0, 8),)),
        "nbr_table": centred(key_list[1], (BLOCKS, NLEN, E), 1.0, 6.0, ((0, 4),)),
        "nbr_ids": draw_nbr_ids(jax.random.fold_in(key_list[11], 71), 0),
        "w_query": centred(key_list[3], (D, D), D ** -0.5, 0.09375, ((1, 4),)),
        "w_key": centred(key_list[4], (E, D), E ** -0.5, 0.1875, ((1, 4),)),
        "w_value": centred(key_list[5], (E, D), E ** -0.5, 0.1875, ((1, 4),)),
        "w_out": bell_draw_with(key_list[6], (D, D), D ** -0.5, 0.125, ((0, 4),), (0, 1, 4, 2.0)),
        "enc_query": centred(key_list[7], (E, E), E ** -0.5, 0.1875),
        "enc_key": centred(key_list[8], (D, E), D ** -0.5, 0.09375, ((0, 8),)),
        "enc_value": centred(key_list[9], (D, E), D ** -0.5, 0.09375, ((0, 8),)),
        "enc_out": centred(key_list[10], (E, E), E ** -0.5, 0.1875),
    }


EPSILON = 1e-06

def encoder_block(sources, cond_keys, cond_values, enc_query, enc_out):
    count = sources.shape[0]
    source_f = sources.astype(jnp.float32)
    normed = (source_f * lax.rsqrt(lax.optimization_barrier(jnp.mean(source_f * source_f, axis=-1, keepdims=True)) + EPSILON)).astype(jnp.bfloat16)
    queries = jnp.dot(normed.reshape(count * NLEN, E), enc_query, preferred_element_type=jnp.float32).astype(jnp.bfloat16)
    queries = queries.reshape(count, NLEN, EHEADS, EHD)
    key_heads = cond_keys.reshape(count, CH, EHEADS, EHD)
    value_heads = cond_values.reshape(count, CH, EHEADS, EHD)
    scores = jnp.einsum('nqhd,nkhd->nhqk', queries.astype(jnp.float32), key_heads.astype(jnp.float32)) / math.sqrt(EHD)
    weights = jax.nn.softmax(scores, axis=-1).astype(jnp.bfloat16)
    mixed_heads = jnp.einsum('nhqk,nkhd->nqhd', weights.astype(jnp.float32), value_heads.astype(jnp.float32)).astype(jnp.bfloat16)
    branch = jnp.dot(mixed_heads.reshape(count * NLEN, E), enc_out, preferred_element_type=jnp.float32)
    return (source_f + branch.reshape(count, NLEN, E)).astype(jnp.bfloat16)

def reference(hidden, nbr_table, nbr_ids, w_query, w_key, w_value, w_out, enc_query, enc_key, enc_value, enc_out):
    cond_keys = jnp.dot(hidden, enc_key, preferred_element_type=jnp.float32).astype(jnp.bfloat16).reshape(SPANS, CH, E)
    cond_values = jnp.dot(hidden, enc_value, preferred_element_type=jnp.float32).astype(jnp.bfloat16).reshape(SPANS, CH, E)
    flat_ids = nbr_ids.reshape(-1).astype(jnp.int32)
    span_of = jnp.arange(SPANS * KNB, dtype=jnp.int32) // KNB
    encoded = encoder_block(nbr_table[flat_ids], cond_keys[span_of], cond_values[span_of], enc_query, enc_out)
    encoded = encoded.reshape(SPANS, KNB * NLEN, E)
    previous = jnp.concatenate([jnp.zeros((1, KNB * NLEN, E), jnp.bfloat16), encoded[:-1]], axis=0)
    queries = jnp.dot(hidden, w_query, preferred_element_type=jnp.float32).astype(jnp.bfloat16)
    queries = queries.reshape(SPANS, CH, HEADS, HD)

    def one_span(pair):
        query_heads, before = pair
        dec_keys = jnp.dot(before, w_key, preferred_element_type=jnp.float32).astype(jnp.bfloat16)
        dec_values = jnp.dot(before, w_value, preferred_element_type=jnp.float32).astype(jnp.bfloat16)
        key_heads = dec_keys.reshape(KNB * NLEN, HEADS, HD).astype(jnp.float32)
        value_heads = dec_values.reshape(KNB * NLEN, HEADS, HD).astype(jnp.float32)
        scores = jnp.einsum('qhd,khd->hqk', query_heads.astype(jnp.float32), key_heads) / math.sqrt(HD)
        weights = jax.nn.softmax(scores, axis=-1).astype(jnp.bfloat16)
        mixed_heads = jnp.einsum('hqk,khd->qhd', weights.astype(jnp.float32), value_heads)
        return mixed_heads.astype(jnp.bfloat16).reshape(CH, D)
    attended = lax.map(one_span, (queries, previous)).reshape(TOKENS, D)
    groups = attended.reshape(TOKENS, N_STORE, HG * HD)
    out_rows = w_out.reshape(N_STORE, HG * HD, D)
    running = jnp.zeros((TOKENS, D), jnp.float32)
    for group in range(N_STORE):
        term = jnp.dot(groups[:, group], out_rows[group], preferred_element_type=jnp.float32)
        running = running + term.astype(jnp.bfloat16).astype(jnp.float32)
    return running.astype(jnp.bfloat16)
```

```python
import functools
import math

import jax
import jax.numpy as jnp
from jax import lax
from jax.experimental import pallas as pl
from jax.experimental.pallas import tpu as pltpu
from jax.sharding import PartitionSpec as P

D = 4096
HD = 128
E = 896
EHD = 64
CH = 64
NLEN = 128
KNB = 2
LANES = 128
E_TILES = E // LANES
EPSILON = 1e-06
CHUNK_SPANS = 4
CHUNK = CHUNK_SPANS * CH
CORES = 2
MESH = pl.DeviceIdType.MESH
F32 = jnp.float32
BF16 = jnp.bfloat16


def dot_nt(a, b):
    return lax.dot_general(a, b, (((1,), (1,)), ((), ())), preferred_element_type=F32)


def dot_tn(a, b):
    return lax.dot_general(a, b, (((0,), (0,)), ((), ())), preferred_element_type=F32)


def dot_nn(a, b):
    return jnp.dot(a, b, preferred_element_type=F32)


def block_diagonal(rows, heads):
    tiled = jnp.concatenate([rows] * heads, axis=0)
    row_head = lax.broadcasted_iota(jnp.int32, tiled.shape, 0) // EHD
    col_head = lax.broadcasted_iota(jnp.int32, tiled.shape, 1) // EHD
    return jnp.where(row_head == col_head, tiled, jnp.zeros_like(tiled))


def encode_span(span, keep, src_ref, encq_ref, cond_ref, enc_out_ref, mixed_ref):
    rows = KNB * NLEN
    at = pl.ds(pl.multiple_of(span * rows, rows), rows)
    tokens = pl.ds(pl.multiple_of(span * CH, CH), CH)
    per_device = cond_ref.shape[2] // LANES

    def cond_tile(tile):
        lane = (tile % per_device) * LANES
        return cond_ref[tile // per_device, tokens, lane : lane + LANES]

    for first in range(0, E_TILES, 2):
        tiles = range(first, min(first + 2, E_TILES))
        heads = len(tiles) * LANES // EHD
        lanes = slice(first * LANES, (first + len(tiles)) * LANES)
        keys = jnp.concatenate([cond_tile(t) for t in tiles], axis=1)
        values = jnp.concatenate([cond_tile(E_TILES + t) for t in tiles], axis=1)
        scores = dot_nt(block_diagonal(keys, heads), encq_ref[at, lanes])
        scores = (scores * (1.0 / math.sqrt(EHD))).reshape(heads, CH, rows)
        exps = jnp.exp(scores - jnp.max(scores, axis=1, keepdims=True))
        weights = exps * (1.0 / jnp.sum(exps, axis=1, keepdims=True))
        weights = weights.astype(BF16).reshape(heads * CH, rows)
        mixed_ref[:, lanes] = dot_tn(weights, block_diagonal(values, heads)).astype(BF16)
    branch = dot_nn(mixed_ref[...], enc_out_ref[...])
    return ((src_ref[at, :].astype(F32) + branch) * keep).astype(BF16)


def decode_span(span, encoded, queries_ref, w_key_ref, w_value_ref, key_ref, value_ref, att_ref, row):
    key_ref[...] = dot_nn(encoded, w_key_ref[...]).astype(BF16)
    value_ref[...] = dot_nn(encoded, w_value_ref[...]).astype(BF16)
    tokens = pl.ds(pl.multiple_of(span * CH, CH), CH)
    out_rows = pl.ds(pl.multiple_of(row * CH, CH), CH)
    for head in range(key_ref.shape[1] // HD):
        lanes = slice(head * HD, (head + 1) * HD)
        scores = dot_nt(queries_ref[tokens, lanes], key_ref[:, lanes]) * (1.0 / math.sqrt(HD))
        exps = jnp.exp(scores - jnp.max(scores, axis=1, keepdims=True))
        weights = exps * (1.0 / jnp.sum(exps, axis=1, keepdims=True))
        att_ref[out_rows, lanes] = dot_nn(weights.astype(BF16), value_ref[:, lanes]).astype(BF16)


def attend_kernel(
    n_store,
    src_ref,
    encq_ref,
    cond_ref,
    queries_ref,
    enc_out_ref,
    w_key_ref,
    w_value_ref,
    w_out_ref,
    out_ref,
    mixed_ref,
    key_ref,
    value_ref,
    att_ref,
    give_ref,
    take_ref,
    pass_ref,
    land_ref,
    pair_ref,
    give_sem,
    take_sem,
    pass_sem,
    land_sem,
):
    seq = lax.axis_index("seq")
    store = lax.axis_index("store")
    chips = n_store // CORES
    chip = store // CORES
    core = store % CORES
    other = chip * CORES + (1 - core)
    width = out_ref.shape[1]
    chunks = out_ref.shape[0] // CHUNK

    def far(step):
        return lax.rem(chip + step, chips)

    barrier = pltpu.get_barrier_semaphore()
    pl.semaphore_signal(barrier, inc=1, device_id=(seq, other), device_id_type=MESH)
    for step in range(1, chips):
        pl.semaphore_signal(
            barrier, inc=1, device_id=(seq, far(step) * CORES + core), device_id_type=MESH
        )
    pl.semaphore_wait(barrier, chips)

    def give(chunk, step):
        return pltpu.make_async_remote_copy(
            src_ref=give_ref.at[chunk, step],
            dst_ref=take_ref.at[chunk, step],
            send_sem=give_sem.at[chunk, step],
            recv_sem=take_sem.at[chunk, step],
            device_id=(seq, other),
            device_id_type=MESH,
        )

    def hand_on(chunk, step):
        return pltpu.make_async_remote_copy(
            src_ref=pass_ref.at[chunk, step - 1],
            dst_ref=land_ref.at[chunk, step - 1],
            send_sem=pass_sem.at[chunk, step - 1],
            recv_sem=land_sem.at[chunk, step - 1],
            device_id=(seq, far(step) * CORES + core),
            device_id_type=MESH,
        )

    def term(chip_at, core_at):
        start = pl.multiple_of((chip_at * CORES + core_at) * width, width)
        return dot_nn(att_ref[...], w_out_ref[:, pl.ds(start, width)])

    @pl.loop(0, chunks)
    def _(chunk):
        @pl.loop(0, CHUNK_SPANS)
        def _(row):
            span = chunk * CHUNK_SPANS + row
            keep = jnp.where((span == 0) & (seq == 0), 0.0, 1.0)
            encoded = encode_span(
                span, keep, src_ref, encq_ref, cond_ref, enc_out_ref, mixed_ref
            )
            decode_span(
                span, encoded, queries_ref, w_key_ref, w_value_ref, key_ref, value_ref, att_ref, row
            )

        for step in range(1, chips + 1):
            slot = step % chips
            give_ref[chunk, slot] = term(far(step), 1 - core).astype(BF16)
            give(chunk, slot).start()
        rows = pl.ds(pl.multiple_of(chunk * CHUNK, CHUNK), CHUNK)
        for step in range(1, chips + 1):
            slot = step % chips
            own = term(far(step), core).astype(BF16).astype(F32)
            give(chunk, slot).wait_recv()
            both = own + take_ref[chunk, slot].astype(F32)
            if slot == 0:
                pair_ref[rows, :] = both
            else:
                pass_ref[chunk, slot - 1] = both.astype(BF16)
                hand_on(chunk, slot).start()

    @pl.loop(0, chunks)
    def _(chunk):
        rows = pl.ds(pl.multiple_of(chunk * CHUNK, CHUNK), CHUNK)
        total = pair_ref[rows, :]
        for step in range(1, chips):
            hand_on(chunk, step).wait_recv()
            total = total + land_ref[chunk, step - 1].astype(F32)
        out_ref[rows, :] = total.astype(BF16)
        for slot in range(chips):
            give(chunk, slot).wait_send()
        for step in range(1, chips):
            hand_on(chunk, step).wait_send()


def attend(n_store, src, encq, cond, queries, enc_out, w_key, w_value, w_out):
    tokens = queries.shape[0]
    head_width = queries.shape[1]
    width = w_out.shape[1] // n_store
    chips = n_store // CORES
    chunks = tokens // CHUNK
    vmem = pl.BlockSpec(memory_space=pltpu.VMEM)
    return pl.pallas_call(
        functools.partial(attend_kernel, n_store),
        out_shape=jax.ShapeDtypeStruct((tokens, width), BF16),
        in_specs=[vmem] * 8,
        out_specs=vmem,
        scratch_shapes=[
            pltpu.VMEM((KNB * NLEN, E), BF16),
            pltpu.VMEM((KNB * NLEN, head_width), BF16),
            pltpu.VMEM((KNB * NLEN, head_width), BF16),
            pltpu.VMEM((CHUNK, head_width), BF16),
            pltpu.VMEM((chunks, chips, CHUNK, width), BF16),
            pltpu.VMEM((chunks, chips, CHUNK, width), BF16),
            pltpu.VMEM((chunks, chips - 1, CHUNK, width), BF16),
            pltpu.VMEM((chunks, chips - 1, CHUNK, width), BF16),
            pltpu.VMEM((tokens, width), F32),
            pltpu.SemaphoreType.DMA((chunks, chips)),
            pltpu.SemaphoreType.DMA((chunks, chips)),
            pltpu.SemaphoreType.DMA((chunks, chips - 1)),
            pltpu.SemaphoreType.DMA((chunks, chips - 1)),
        ],
        compiler_params=pltpu.CompilerParams(
            collective_id=1, has_side_effects=True, vmem_limit_bytes=62 * 2**20
        ),
        name="attend",
    )(src, encq, cond, queries, enc_out, w_key, w_value, w_out)


def shifted(block, axis, distance):
    devices = range(lax.axis_size(axis))
    route = [(i - distance, i) for i in devices if i - distance in devices]
    return lax.ppermute(block, axis, route)


def body(
    hidden,
    nbr_table,
    nbr_ids,
    w_query,
    w_key,
    w_value,
    w_out,
    enc_query,
    enc_key,
    enc_value,
    enc_out,
):
    n_store = lax.axis_size("store")
    store = lax.axis_index("store")
    own_width = -(-2 * E_TILES // n_store) * LANES
    padding = own_width * n_store - 2 * E
    enc_kv = jnp.concatenate(
        [enc_key, enc_value, jnp.zeros((enc_key.shape[0], padding), BF16)], axis=1
    )
    own_kv = lax.dynamic_slice_in_dim(enc_kv, store * own_width, own_width, axis=1)
    all_kv = lax.all_gather(own_kv, "seq", axis=0, tiled=True)
    table = lax.all_gather(nbr_table, "store", axis=0, tiled=True)
    ids = jnp.concatenate([shifted(nbr_ids[-1:], "seq", 1), nbr_ids[:-1]], axis=0)
    src = table[ids.reshape(-1)].reshape(-1, E)
    src_f = src.astype(F32)
    normed = (
        src_f * lax.rsqrt(jnp.mean(src_f * src_f, axis=-1, keepdims=True) + EPSILON)
    ).astype(BF16)
    encq = dot_nn(normed, enc_query).astype(BF16)
    queries = dot_nn(hidden, w_query).astype(BF16)
    own_cond = dot_nn(hidden, all_kv).astype(BF16)
    own_cond = jnp.concatenate([shifted(own_cond[-CH:], "seq", 1), own_cond[:-CH]], axis=0)
    cond = lax.all_gather(own_cond, "store", axis=0, tiled=False)
    return attend(n_store, src, encq, cond, queries, enc_out, w_key, w_value, w_out)


def solution(mesh):
    in_specs = (
        P("seq", None),
        P("store", None, None),
        P("seq", None),
        P(None, "store"),
        P(None, "store"),
        P(None, "store"),
        P("store", None),
        P(),
        P("seq", None),
        P("seq", None),
        P(),
    )
    out_specs = P("seq", "store")
    return jax.shard_map(body, mesh=mesh, in_specs=in_specs, out_specs=out_specs, check_vma=False)
```

```python
import functools
import math

import jax
import jax.numpy as jnp
from jax import lax
from jax.experimental import pallas as pl
from jax.experimental.pallas import tpu as pltpu
from jax.sharding import PartitionSpec as P

D = 4096
HD = 128
E = 896
EHD = 64
CH = 64
NLEN = 128
KNB = 2
LANES = 128
E_TILES = E // LANES
EPSILON = 1e-06
CHUNK_SPANS = 4
CHUNK = CHUNK_SPANS * CH
CORES = 2
LOG2E = math.log2(math.e)
MESH = pl.DeviceIdType.MESH
F32 = jnp.float32
BF16 = jnp.bfloat16


def dot_nt(a, b):
    return lax.dot_general(a, b, (((1,), (1,)), ((), ())), preferred_element_type=F32)


def dot_tn(a, b):
    return lax.dot_general(a, b, (((0,), (0,)), ((), ())), preferred_element_type=F32)


def dot_nn(a, b):
    return jnp.dot(a, b, preferred_element_type=F32)


def block_diagonal(rows, heads):
    tiled = jnp.concatenate([rows] * heads, axis=0)
    row_head = lax.broadcasted_iota(jnp.int32, tiled.shape, 0) // EHD
    col_head = lax.broadcasted_iota(jnp.int32, tiled.shape, 1) // EHD
    return jnp.where(row_head == col_head, tiled, jnp.zeros_like(tiled))


def mix_span(span, row, encq_ref, cond_ref, mixed_ref):
    rows = KNB * NLEN
    at = pl.ds(pl.multiple_of(span * rows, rows), rows)
    out_rows = pl.ds(pl.multiple_of(row * rows, rows), rows)
    tokens = pl.ds(pl.multiple_of(span * CH, CH), CH)
    per_device = cond_ref.shape[2] // LANES

    def cond_tile(tile):
        lane = (tile % per_device) * LANES
        return cond_ref[tile // per_device, tokens, lane : lane + LANES]

    for first in range(0, E_TILES, 2):
        tiles = range(first, min(first + 2, E_TILES))
        heads = len(tiles) * LANES // EHD
        lanes = slice(first * LANES, (first + len(tiles)) * LANES)
        keys = jnp.concatenate([cond_tile(t) for t in tiles], axis=1)
        values = jnp.concatenate([cond_tile(E_TILES + t) for t in tiles], axis=1)
        scores = dot_nt(block_diagonal(keys, heads), encq_ref[at, lanes])
        scores = scores.reshape(heads, CH, rows)
        scores = scores - jnp.max(scores, axis=1, keepdims=True)
        exps = jnp.exp2(scores * (LOG2E / math.sqrt(EHD)))
        weights = exps * (1.0 / jnp.sum(exps, axis=1, keepdims=True))
        weights = weights.astype(BF16).reshape(heads * CH, rows)
        mixed_ref[out_rows, lanes] = dot_tn(weights, block_diagonal(values, heads)).astype(BF16)


def decode_span(span, row, queries_ref, key_ref, value_ref, att_ref):
    rows = pl.ds(pl.multiple_of(row * KNB * NLEN, KNB * NLEN), KNB * NLEN)
    tokens = pl.ds(pl.multiple_of(span * CH, CH), CH)
    out_rows = pl.ds(pl.multiple_of(row * CH, CH), CH)
    for head in range(key_ref.shape[1] // HD):
        lanes = slice(head * HD, (head + 1) * HD)
        scores = dot_nt(queries_ref[tokens, lanes], key_ref[rows, lanes])
        scores = scores - jnp.max(scores, axis=1, keepdims=True)
        exps = jnp.exp2(scores * (LOG2E / math.sqrt(HD)))
        mixed = dot_nn(exps.astype(BF16), value_ref[rows, lanes])
        scale = 1.0 / jnp.sum(exps, axis=1, keepdims=True)
        att_ref[out_rows, lanes] = (mixed * scale).astype(BF16)


def attend_kernel(
    n_store,
    src_hbm,
    encq_hbm,
    cond_hbm,
    queries_hbm,
    enc_out_hbm,
    w_key_hbm,
    w_value_hbm,
    w_out_hbm,
    out_ref,
    src_ref,
    encq_ref,
    cond_ref,
    queries_ref,
    enc_out_ref,
    w_key_ref,
    w_value_ref,
    w_out_ref,
    mixed_ref,
    key_ref,
    value_ref,
    att_ref,
    give_ref,
    take_ref,
    pass_ref,
    land_ref,
    pair_ref,
    load_sem,
    give_sem,
    take_sem,
    pass_sem,
    land_sem,
):
    loads = [
        pltpu.make_async_copy(source, target, load_sem.at[at])
        for at, (source, target) in enumerate(
            (
                (encq_hbm, encq_ref),
                (cond_hbm, cond_ref),
                (src_hbm, src_ref),
                (enc_out_hbm, enc_out_ref),
                (w_key_hbm, w_key_ref),
                (w_value_hbm, w_value_ref),
                (queries_hbm, queries_ref),
                (w_out_hbm, w_out_ref),
            )
        )
    ]
    for copy in loads:
        copy.start()
    seq = lax.axis_index("seq")
    store = lax.axis_index("store")
    chips = n_store // CORES
    chip = store // CORES
    core = store % CORES
    other = chip * CORES + (1 - core)
    width = out_ref.shape[1]
    chunks = out_ref.shape[0] // CHUNK

    def far(step):
        return lax.rem(chip + step, chips)

    barrier = pltpu.get_barrier_semaphore()
    pl.semaphore_signal(barrier, inc=1, device_id=(seq, other), device_id_type=MESH)
    for step in range(1, chips):
        pl.semaphore_signal(
            barrier, inc=1, device_id=(seq, far(step) * CORES + core), device_id_type=MESH
        )
    pl.semaphore_wait(barrier, chips)

    def give(chunk, step):
        return pltpu.make_async_remote_copy(
            src_ref=give_ref.at[chunk, step],
            dst_ref=take_ref.at[chunk, step],
            send_sem=give_sem.at[chunk, step],
            recv_sem=take_sem.at[chunk, step],
            device_id=(seq, other),
            device_id_type=MESH,
        )

    def hand_on(chunk, step):
        return pltpu.make_async_remote_copy(
            src_ref=pass_ref.at[chunk, step - 1],
            dst_ref=land_ref.at[chunk, step - 1],
            send_sem=pass_sem.at[chunk, step - 1],
            recv_sem=land_sem.at[chunk, step - 1],
            device_id=(seq, far(step) * CORES + core),
            device_id_type=MESH,
        )

    def term(chip_at, core_at):
        start = pl.multiple_of((chip_at * CORES + core_at) * width, width)
        return dot_nn(att_ref[...], w_out_ref[:, pl.ds(start, width)])

    def arrived(chunk, which):
        @pl.when(chunk == 0)
        def _():
            for copy in which:
                copy.wait()

    rows_all = KNB * NLEN * CHUNK_SPANS

    @pl.loop(0, chunks)
    def _(chunk):
        arrived(chunk, loads[:2])

        @pl.loop(0, CHUNK_SPANS // 2)
        def _(pair):
            for row in (2 * pair, 2 * pair + 1):
                mix_span(chunk * CHUNK_SPANS + row, row, encq_ref, cond_ref, mixed_ref)

        arrived(chunk, loads[2:4])

        @pl.loop(0, 2)
        def _(half):
            rows = pl.ds(pl.multiple_of(half * (rows_all // 2), rows_all // 2), rows_all // 2)
            source_at = pl.multiple_of(chunk * rows_all + half * (rows_all // 2), rows_all // 2)
            branch = dot_nn(mixed_ref[rows, :], enc_out_ref[...])
            source = src_ref[pl.ds(source_at, rows_all // 2), :].astype(F32)
            mixed_ref[rows, :] = (source + branch).astype(BF16)

        @pl.when((chunk == 0) & (seq == 0))
        def _():
            mixed_ref[: KNB * NLEN, :] = jnp.zeros((KNB * NLEN, E), BF16)

        arrived(chunk, loads[4:6])
        span_width = key_ref.shape[1] // 2

        @pl.loop(0, 2)
        def _(half):
            lanes = pl.ds(pl.multiple_of(half * span_width, span_width), span_width)
            key_ref[:, lanes] = dot_nn(mixed_ref[...], w_key_ref[:, lanes]).astype(BF16)
            value_ref[:, lanes] = dot_nn(mixed_ref[...], w_value_ref[:, lanes]).astype(BF16)

        arrived(chunk, loads[6:7])

        @pl.loop(0, CHUNK_SPANS // 2)
        def _(pair):
            for row in (2 * pair, 2 * pair + 1):
                decode_span(
                    chunk * CHUNK_SPANS + row, row, queries_ref, key_ref, value_ref, att_ref
                )

        arrived(chunk, loads[7:])

        for step in range(1, chips + 1):
            slot = step % chips
            give_ref[chunk, slot] = term(far(step), 1 - core).astype(BF16)
            give(chunk, slot).start()
        rows = pl.ds(pl.multiple_of(chunk * CHUNK, CHUNK), CHUNK)
        for step in range(1, chips + 1):
            slot = step % chips
            own = term(far(step), core).astype(BF16).astype(F32)
            give(chunk, slot).wait_recv()
            both = own + take_ref[chunk, slot].astype(F32)
            if slot == 0:
                pair_ref[rows, :] = both
            else:
                pass_ref[chunk, slot - 1] = both.astype(BF16)
                hand_on(chunk, slot).start()

    @pl.loop(0, chunks)
    def _(chunk):
        rows = pl.ds(pl.multiple_of(chunk * CHUNK, CHUNK), CHUNK)
        total = pair_ref[rows, :]
        for step in range(1, chips):
            hand_on(chunk, step).wait_recv()
            total = total + land_ref[chunk, step - 1].astype(F32)
        out_ref[rows, :] = total.astype(BF16)
        for slot in range(chips):
            give(chunk, slot).wait_send()
        for step in range(1, chips):
            hand_on(chunk, step).wait_send()


def attend(n_store, src, encq, cond, queries, enc_out, w_key, w_value, w_out):
    tokens = queries.shape[0]
    head_width = queries.shape[1]
    width = w_out.shape[1] // n_store
    chips = n_store // CORES
    chunks = tokens // CHUNK
    rows = KNB * NLEN * CHUNK_SPANS
    operands = (src, encq, cond, queries, enc_out, w_key, w_value, w_out)
    vmem = pl.BlockSpec(memory_space=pltpu.VMEM)
    return pl.pallas_call(
        functools.partial(attend_kernel, n_store),
        out_shape=jax.ShapeDtypeStruct((tokens, width), BF16),
        in_specs=[pl.BlockSpec(memory_space=pl.ANY)] * 8,
        out_specs=vmem,
        scratch_shapes=[pltpu.VMEM(operand.shape, BF16) for operand in operands]
        + [
            pltpu.VMEM((rows, E), BF16),
            pltpu.VMEM((rows, head_width), BF16),
            pltpu.VMEM((rows, head_width), BF16),
            pltpu.VMEM((CHUNK, head_width), BF16),
            pltpu.VMEM((chunks, chips, CHUNK, width), BF16),
            pltpu.VMEM((chunks, chips, CHUNK, width), BF16),
            pltpu.VMEM((chunks, chips - 1, CHUNK, width), BF16),
            pltpu.VMEM((chunks, chips - 1, CHUNK, width), BF16),
            pltpu.VMEM((tokens, width), F32),
            pltpu.SemaphoreType.DMA((len(operands),)),
            pltpu.SemaphoreType.DMA((chunks, chips)),
            pltpu.SemaphoreType.DMA((chunks, chips)),
            pltpu.SemaphoreType.DMA((chunks, chips - 1)),
            pltpu.SemaphoreType.DMA((chunks, chips - 1)),
        ],
        compiler_params=pltpu.CompilerParams(
            collective_id=1, has_side_effects=True, vmem_limit_bytes=62 * 2**20
        ),
        name="attend",
    )(*operands)


def front_kernel(
    outer,
    inner,
    n_store,
    hidden_ref,
    w_query_ref,
    kv_ref,
    nbr_ref,
    ids_ref,
    enc_query_ref,
    queries_out,
    src_out,
    encq_out,
    cond_out,
    hidden_v,
    w_query_v,
    queries_v,
    kv_v,
    acc_v,
    own_v,
    zero_v,
    table_v,
    src_v,
    encq_v,
    load_sem,
    kv_send,
    kv_recv,
    table_pair,
    table_far,
    table_recv,
    cond_pair,
    cond_far,
    cond_recv,
    tail_sem,
):
    seq = lax.axis_index("seq")
    store = lax.axis_index("store")
    n_seq = outer * inner
    a, b = seq // inner, seq % inner
    chips = n_store // CORES
    chip, core = store // CORES, store % CORES
    other = chip * CORES + (1 - core)
    blocks = nbr_ref.shape[0]
    depth = kv_ref.shape[0]
    tokens = hidden_ref.shape[0]
    pieces = tokens // CHUNK
    requests = ids_ref.shape[0]
    has_left, has_right = a > 0, a + 1 < outer
    has_low, has_high = b > 0, b + 1 < inner
    has_next, has_prev = seq + 1 < n_seq, seq > 0

    def far(step):
        return lax.rem(chip + step, chips) * CORES + core

    def far_from(step):
        return lax.rem(chip + chips - step, chips) * CORES + core

    barrier = pltpu.get_barrier_semaphore()

    def greet(seq_at, store_at):
        pl.semaphore_signal(barrier, inc=1, device_id=(seq_at, store_at), device_id_type=MESH)

    greetings = chips
    greet(seq, other)
    for step in range(1, chips):
        greet(seq, far(step))
    for there, target in (
        (has_left, seq - inner),
        (has_right, seq + inner),
        (has_low, seq - 1),
        (has_high, seq + 1),
        (has_next, seq + 1),
        (has_prev, seq - 1),
    ):
        greetings = greetings + there.astype(jnp.int32)

        @pl.when(there)
        def _():
            greet(target, store)

    pl.semaphore_wait(barrier, greetings)

    def load(source, target, at):
        return pltpu.make_async_copy(source, target, load_sem.at[at])

    def kv_copy(slot, way, source=None):
        target = (seq - inner, seq + inner, seq - 1, seq + 1)[way]
        return pltpu.make_async_remote_copy(
            src_ref=kv_v.at[slot] if source is None else source,
            dst_ref=kv_v.at[slot],
            send_sem=kv_send.at[slot, way],
            recv_sem=kv_recv.at[slot],
            device_id=(target, store),
            device_id_type=MESH,
        )

    ways = (has_left, has_right, has_low, has_high)

    def send_kv(slot, which, source=None):
        for way in which:

            @pl.when(ways[way])
            def _():
                kv_copy(slot, way, source).start()

    def table_copy(owner, target, sem, source=None):
        at = table_v.at[pl.ds(owner * blocks, blocks)]
        return pltpu.make_async_remote_copy(
            src_ref=at if source is None else source,
            dst_ref=at,
            send_sem=sem,
            recv_sem=table_recv.at[owner],
            device_id=(seq, target),
            device_id_type=MESH,
        )

    def table_to_pair(owner, source=None):
        return table_copy(owner, other, table_pair.at[owner], source)

    def table_to_far(step):
        return table_copy(store, far(step), table_far.at[step - 1], nbr_ref)

    def cond_copy(piece, owner, target, sem, source=None):
        at = cond_out.at[owner, pl.ds(piece * CHUNK, CHUNK)]
        return pltpu.make_async_remote_copy(
            src_ref=at if source is None else source,
            dst_ref=at,
            send_sem=sem,
            recv_sem=cond_recv.at[piece, owner],
            device_id=(seq, target),
            device_id_type=MESH,
        )

    def cond_to_pair(piece, owner, source=None):
        return cond_copy(piece, owner, other, cond_pair.at[piece, owner], source)

    def cond_to_far(piece, step, source=None):
        return cond_copy(piece, store, far(step), cond_far.at[piece, step - 1], source)

    send_kv(seq, (0, 1, 2, 3), kv_ref)
    for step in range(1, chips):
        table_to_far(step).start()
    table_to_pair(store, nbr_ref).start()
    own_kv = load(kv_ref, kv_v.at[seq], 0)
    own_table = load(nbr_ref, table_v.at[pl.ds(store * blocks, blocks)], 1)
    hidden_load = load(hidden_ref, hidden_v, 2)
    query_load = load(w_query_ref, w_query_v, 3)
    for copy in (own_kv, hidden_load, query_load, own_table):
        copy.start()
    own_kv.wait()
    hidden_load.wait()

    def accumulate(slot, first=False):
        @pl.loop(0, pieces)
        def _(piece):
            rows = pl.ds(pl.multiple_of(piece * CHUNK, CHUNK), CHUNK)
            part = hidden_v[rows, pl.ds(pl.multiple_of(slot * depth, depth), depth)]
            product = dot_nn(part, kv_v[slot])
            if first:
                acc_v[rows, :] = product
            else:
                acc_v[rows, :] += product

    accumulate(seq, first=True)
    query_load.wait()
    query_rows = tokens // outer
    query_width = queries_v.shape[1] // 2

    @pl.loop(0, outer)
    def _(step):
        rows = pl.ds(pl.multiple_of(step * query_rows, query_rows), query_rows)

        @pl.loop(0, 2)
        def _(half):
            lanes = pl.ds(pl.multiple_of(half * query_width, query_width), query_width)
            queries_v[rows, lanes] = dot_nn(hidden_v[rows, :], w_query_v[:, lanes]).astype(BF16)

        from_left = (step > 0) & (a >= step)
        from_right = (step > 0) & (a + step < outer)
        left_slot = seq - step * inner
        right_slot = seq + step * inner

        @pl.when(from_left)
        def _():
            kv_copy(left_slot, 1).wait_recv()
            send_kv(left_slot, (1, 2, 3))

        @pl.when(from_right)
        def _():
            kv_copy(right_slot, 0).wait_recv()
            send_kv(right_slot, (0, 2, 3))

        @pl.when(from_left)
        def _():
            accumulate(left_slot)

        @pl.when(from_right)
        def _():
            accumulate(right_slot)

    queries_store = load(queries_v, queries_out, 3)
    queries_store.start()
    toward = jnp.where(2 * a < outer, 1, -1)

    @pl.loop(1, inner)
    def _(step):
        @pl.loop(0, outer)
        def _(count):
            line = lax.rem(a + toward * count + outer, outer) * inner + b

            @pl.when(b >= step)
            def _():
                kv_copy(line - step, 3).wait_recv()
                send_kv(line - step, (3,))
                accumulate(line - step)

            @pl.when(b + step < inner)
            def _():
                kv_copy(line + step, 2).wait_recv()
                send_kv(line + step, (2,))
                accumulate(line + step)

    @pl.loop(0, pieces)
    def _(piece):
        rows = pl.ds(pl.multiple_of(piece * CHUNK, CHUNK), CHUNK)
        own_v[rows, :] = acc_v[rows, :].astype(BF16)

    tail = pltpu.make_async_remote_copy(
        src_ref=own_v.at[pl.ds(tokens - CH, CH)],
        dst_ref=cond_out.at[store, pl.ds(0, CH)],
        send_sem=tail_sem.at[0],
        recv_sem=tail_sem.at[1],
        device_id=(seq + 1, store),
        device_id_type=MESH,
    )

    @pl.when(has_next)
    def _():
        tail.start()

    for piece in range(1, pieces):
        source = own_v.at[pl.ds(piece * CHUNK - CH, CHUNK)]
        for step in range(1, chips):
            cond_to_far(piece, step, source).start()
        cond_to_pair(piece, store, source).start()
    body_copy = load(
        own_v.at[pl.ds(0, tokens - CH)], cond_out.at[store, pl.ds(CH, tokens - CH)], 0
    )
    body_copy.start()
    zero_copy = load(zero_v, cond_out.at[store, pl.ds(0, CH)], 2)

    @pl.when(has_prev)
    def _():
        tail.wait_recv()

    @pl.when(jnp.logical_not(has_prev))
    def _():
        zero_v[...] = jnp.zeros_like(zero_v)
        zero_copy.start()
        zero_copy.wait()

    body_copy.wait()
    for step in range(1, chips):
        cond_to_far(0, step).start()
    cond_to_pair(0, store).start()

    own_table.wait()
    for step in range(1, chips):
        table_to_pair(far_from(step)).wait_recv()
        table_to_pair(far_from(step)).start()
    table_to_pair(other).wait_recv()
    for step in range(1, chips):
        mirrored = far_from(step) + 1 - 2 * core
        table_to_pair(mirrored).wait_recv()

    @pl.loop(0, requests // KNB)
    def _(pair):
        for part in range(KNB):
            request = pair * KNB + part
            rows = pl.ds(pl.multiple_of(request * NLEN, NLEN), NLEN)
            block = table_v[ids_ref[request]]
            src_v[rows, :] = block
            block = block.astype(F32)
            mean = jnp.mean(block * block, axis=-1, keepdims=True)
            encq_v[rows, :] = (block * lax.rsqrt(mean + EPSILON)).astype(BF16)
        both = pl.ds(pl.multiple_of(pair * KNB * NLEN, KNB * NLEN), KNB * NLEN)
        encq_v[both, :] = dot_nn(encq_v[both, :], enc_query_ref[...]).astype(BF16)

    src_store = load(src_v, src_out, 1)
    encq_store = load(encq_v, encq_out, 2)
    src_store.start()
    encq_store.start()

    order = tuple(range(1, pieces)) + (0,)
    for piece in order:
        for step in range(1, chips):
            cond_to_pair(piece, far_from(step)).wait_recv()
            cond_to_pair(piece, far_from(step)).start()
    for piece in order:
        cond_to_pair(piece, other).wait_recv()
        for step in range(1, chips):
            cond_to_pair(piece, far_from(step) + 1 - 2 * core).wait_recv()

    @pl.when(has_next)
    def _():
        tail.wait_send()

    for piece in order:
        cond_to_pair(piece, store).wait_send()
        for step in range(1, chips):
            cond_to_far(piece, step).wait_send()
            cond_to_pair(piece, far_from(step)).wait_send()
    table_to_pair(store).wait_send()
    for step in range(1, chips):
        table_to_far(step).wait_send()
        table_to_pair(far_from(step)).wait_send()

    def sent(slot, which):
        for way in which:

            @pl.when(ways[way])
            def _():
                kv_copy(slot, way).wait_send()

    @pl.loop(0, outer)
    def _(step):
        @pl.when(step == 0)
        def _():
            sent(seq, (0, 1, 2, 3))

        @pl.when((step > 0) & (a >= step))
        def _():
            sent(seq - step * inner, (1, 2, 3))

        @pl.when((step > 0) & (a + step < outer))
        def _():
            sent(seq + step * inner, (0, 2, 3))

    @pl.loop(1, inner)
    def _(step):
        @pl.loop(0, outer)
        def _(line):
            @pl.when(b >= step)
            def _():
                sent(line * inner + b - step, (3,))

            @pl.when(b + step < inner)
            def _():
                sent(line * inner + b + step, (2,))

    queries_store.wait()
    src_store.wait()
    encq_store.wait()


def front(n_seq, n_store, hidden, w_query, own_kv, nbr_table, ids, enc_query):
    outer = 4
    inner = n_seq // outer
    tokens = hidden.shape[0]
    head_width = w_query.shape[1]
    depth, width = own_kv.shape
    blocks = nbr_table.shape[0] * n_store
    rows = ids.shape[0] * NLEN
    chips = n_store // CORES
    pieces = tokens // CHUNK
    hbm = pl.BlockSpec(memory_space=pl.ANY)
    vmem = pl.BlockSpec(memory_space=pltpu.VMEM)
    smem = pl.BlockSpec(memory_space=pltpu.SMEM)
    dma = pltpu.SemaphoreType.DMA
    return pl.pallas_call(
        functools.partial(front_kernel, outer, inner, n_store),
        out_shape=(
            jax.ShapeDtypeStruct((tokens, head_width), BF16),
            jax.ShapeDtypeStruct((rows, E), BF16),
            jax.ShapeDtypeStruct((rows, E), BF16),
            jax.ShapeDtypeStruct((n_store, tokens, width), BF16),
        ),
        in_specs=[hbm] * 4 + [smem, vmem],
        out_specs=(hbm,) * 4,
        scratch_shapes=[
            pltpu.VMEM(hidden.shape, BF16),
            pltpu.VMEM(w_query.shape, BF16),
            pltpu.VMEM((tokens, head_width), BF16),
            pltpu.VMEM((n_seq, depth, width), BF16),
            pltpu.VMEM((tokens, width), F32),
            pltpu.VMEM((tokens, width), BF16),
            pltpu.VMEM((CH, width), BF16),
            pltpu.VMEM((blocks, NLEN, E), BF16),
            pltpu.VMEM((rows, E), BF16),
            pltpu.VMEM((rows, E), BF16),
            dma((4,)),
            dma((n_seq, 4)),
            dma((n_seq,)),
            dma((n_store,)),
            dma((chips - 1,)),
            dma((n_store,)),
            dma((pieces, n_store)),
            dma((pieces, chips - 1)),
            dma((pieces, n_store)),
            dma((2,)),
        ],
        compiler_params=pltpu.CompilerParams(
            collective_id=2, has_side_effects=True, vmem_limit_bytes=62 * 2**20
        ),
        name="front",
    )(hidden, w_query, own_kv, nbr_table, ids, enc_query)


def shifted(block, axis, distance):
    devices = range(lax.axis_size(axis))
    route = [(i - distance, i) for i in devices if i - distance in devices]
    return lax.ppermute(block, axis, route)


def body(
    hidden,
    nbr_table,
    nbr_ids,
    w_query,
    w_key,
    w_value,
    w_out,
    enc_query,
    enc_key,
    enc_value,
    enc_out,
):
    n_store = lax.axis_size("store")
    store = lax.axis_index("store")
    own_width = -(-2 * E_TILES // n_store) * LANES
    padding = own_width * n_store - 2 * E
    enc_kv = jnp.concatenate(
        [enc_key, enc_value, jnp.zeros((enc_key.shape[0], padding), BF16)], axis=1
    )
    own_kv = lax.dynamic_slice_in_dim(enc_kv, store * own_width, own_width, axis=1)
    ids = jnp.concatenate([shifted(nbr_ids[-1:], "seq", 1), nbr_ids[:-1]], axis=0)
    queries, src, encq, cond = front(
        lax.axis_size("seq"), n_store, hidden, w_query, own_kv, nbr_table, ids.reshape(-1), enc_query
    )
    return attend(n_store, src, encq, cond, queries, enc_out, w_key, w_value, w_out)


def solution(mesh):
    in_specs = (
        P("seq", None),
        P("store", None, None),
        P("seq", None),
        P(None, "store"),
        P(None, "store"),
        P(None, "store"),
        P("store", None),
        P(),
        P("seq", None),
        P("seq", None),
        P(),
    )
    out_specs = P("seq", "store")
    return jax.shard_map(body, mesh=mesh, in_specs=in_specs, out_specs=out_specs, check_vma=False)
```

```python
import functools
import math

import jax
import jax.numpy as jnp
from jax import lax
from jax.experimental import pallas as pl
from jax.experimental.pallas import tpu as pltpu
from jax.sharding import PartitionSpec as P

D = 4096
HD = 128
E = 896
EHD = 64
CH = 64
NLEN = 128
KNB = 2
LANES = 128
E_TILES = E // LANES
EPSILON = 1e-06
CHUNK_SPANS = 4
CHUNK = CHUNK_SPANS * CH
CORES = 2
LOG2E = math.log2(math.e)
MESH = pl.DeviceIdType.MESH
F32 = jnp.float32
BF16 = jnp.bfloat16


def dot_nt(a, b):
    return lax.dot_general(a, b, (((1,), (1,)), ((), ())), preferred_element_type=F32)


def dot_tn(a, b):
    return lax.dot_general(a, b, (((0,), (0,)), ((), ())), preferred_element_type=F32)


def dot_nn(a, b):
    return jnp.dot(a, b, preferred_element_type=F32)


def block_diagonal(rows, heads):
    tiled = jnp.concatenate([rows] * heads, axis=0)
    row_head = lax.broadcasted_iota(jnp.int32, tiled.shape, 0) // EHD
    col_head = lax.broadcasted_iota(jnp.int32, tiled.shape, 1) // EHD
    return jnp.where(row_head == col_head, tiled, jnp.zeros_like(tiled))


def mix_span(span, at_span, row, encq_ref, cond_ref, mixed_ref):
    rows = KNB * NLEN
    at = pl.ds(pl.multiple_of(at_span * rows, rows), rows)
    out_rows = pl.ds(pl.multiple_of(row * rows, rows), rows)
    tokens = pl.ds(pl.multiple_of(span * CH, CH), CH)
    per_device = cond_ref.shape[2] // LANES

    def cond_tile(tile):
        lane = (tile % per_device) * LANES
        return cond_ref[tile // per_device, tokens, lane : lane + LANES]

    for first in range(0, E_TILES, 2):
        tiles = range(first, min(first + 2, E_TILES))
        heads = len(tiles) * LANES // EHD
        lanes = slice(first * LANES, (first + len(tiles)) * LANES)
        keys = jnp.concatenate([cond_tile(t) for t in tiles], axis=1)
        values = jnp.concatenate([cond_tile(E_TILES + t) for t in tiles], axis=1)
        scores = dot_nt(block_diagonal(keys, heads), encq_ref[at, lanes])
        scores = scores.reshape(heads, CH, rows)
        scores = scores - jnp.max(scores, axis=1, keepdims=True)
        exps = jnp.exp2(scores * (LOG2E / math.sqrt(EHD)))
        weights = exps * (1.0 / jnp.sum(exps, axis=1, keepdims=True))
        weights = weights.astype(BF16).reshape(heads * CH, rows)
        mixed_ref[out_rows, lanes] = dot_tn(weights, block_diagonal(values, heads)).astype(BF16)


def decode_span(row, keep_at, encoded_ref, asks_ref, blend_ref):
    rows = pl.ds(pl.multiple_of(row * KNB * NLEN, KNB * NLEN), KNB * NLEN)
    out_rows = pl.ds(pl.multiple_of(row * CH, CH), CH)
    encoded = encoded_ref[keep_at, rows, :]
    scores = dot_nt(asks_ref[row], encoded)
    scores = scores - jnp.max(scores, axis=1, keepdims=True)
    exps = jnp.exp2(scores * (LOG2E / math.sqrt(HD)))
    scale = 1.0 / jnp.sum(exps, axis=1, keepdims=True)
    blend = (dot_nn(exps.astype(BF16), encoded) * scale).astype(BF16)
    for head in range(blend_ref.shape[0]):
        blend_ref[head, out_rows, :] = blend[head * CH : (head + 1) * CH]


def attend_kernel(
    n_store,
    src_hbm,
    encq_hbm,
    cond_hbm,
    enc_out_hbm,
    w_value_hbm,
    w_out_hbm,
    asks_hbm,
    out_ref,
    src_ref,
    encq_ref,
    cond_ref,
    enc_out_ref,
    w_value_ref,
    w_out_ref,
    asks_ref,
    mixed_ref,
    encoded_ref,
    blend_ref,
    att_ref,
    give_ref,
    take_ref,
    pass_ref,
    land_ref,
    load_sem,
    asks_sem,
    encoded_send,
    encoded_recv,
    give_sem,
    take_sem,
    pass_sem,
    land_sem,
):
    loads = [
        pltpu.make_async_copy(source, target, load_sem.at[at])
        for at, (source, target) in enumerate(
            (
                (encq_hbm, encq_ref),
                (cond_hbm, cond_ref),
                (src_hbm, src_ref),
                (enc_out_hbm, enc_out_ref),
                (w_value_hbm, w_value_ref),
                (w_out_hbm, w_out_ref),
            )
        )
    ]

    def load_asks(chunk):
        return pltpu.make_async_copy(
            asks_hbm.at[pl.ds(chunk * CHUNK_SPANS, CHUNK_SPANS)],
            asks_ref.at[chunk % 2],
            asks_sem.at[chunk % 2],
        )

    for copy in loads[:4]:
        copy.start()
    load_asks(0).start()
    for copy in loads[4:]:
        copy.start()
    seq = lax.axis_index("seq")
    store = lax.axis_index("store")
    chips = n_store // CORES
    chip = store // CORES
    core = store % CORES
    other = chip * CORES + (1 - core)
    width = out_ref.shape[1]
    chunks = out_ref.shape[0] // CHUNK

    def far(step):
        return lax.rem(chip + step, chips)

    barrier = pltpu.get_barrier_semaphore()
    pl.semaphore_signal(barrier, inc=1, device_id=(seq, other), device_id_type=MESH)
    for step in range(1, chips):
        pl.semaphore_signal(
            barrier, inc=1, device_id=(seq, far(step) * CORES + core), device_id_type=MESH
        )
    pl.semaphore_wait(barrier, chips)

    def give(chunk, step):
        return pltpu.make_async_remote_copy(
            src_ref=give_ref.at[chunk, step],
            dst_ref=take_ref.at[chunk, step],
            send_sem=give_sem.at[chunk, step],
            recv_sem=take_sem.at[chunk, step],
            device_id=(seq, other),
            device_id_type=MESH,
        )

    def hand_on(chunk, step):
        return pltpu.make_async_remote_copy(
            src_ref=pass_ref.at[chunk, step - 1],
            dst_ref=land_ref.at[chunk, step - 1],
            send_sem=pass_sem.at[chunk, step - 1],
            recv_sem=land_sem.at[chunk, step - 1],
            device_id=(seq, far(step) * CORES + core),
            device_id_type=MESH,
        )

    def term(chip_at, core_at):
        start = pl.multiple_of((chip_at * CORES + core_at) * width, width)
        return dot_nn(att_ref[...], w_out_ref[:, pl.ds(start, width)])

    span_rows = KNB * NLEN
    half_spans = CHUNK_SPANS // CORES
    half_rows = half_spans * span_rows

    def share(chunk):
        at = encoded_ref.at[chunk, pl.ds(pl.multiple_of(core * half_rows, half_rows), half_rows)]
        return pltpu.make_async_remote_copy(
            src_ref=at,
            dst_ref=at,
            send_sem=encoded_send.at[chunk],
            recv_sem=encoded_recv.at[chunk],
            device_id=(seq, other),
            device_id_type=MESH,
        )

    def encode(chunk):
        @pl.when(chunk == 0)
        def _():
            for copy in loads[:4]:
                copy.wait()

        for row in range(half_spans):
            span = chunk * CHUNK_SPANS + core * half_spans + row
            mix_span(span, chunk * half_spans + row, row, encq_ref, cond_ref, mixed_ref)
        branch = dot_nn(mixed_ref[...], enc_out_ref[...])
        source_at = pl.ds(pl.multiple_of(chunk * half_rows, half_rows), half_rows)
        rows = pl.ds(pl.multiple_of(core * half_rows, half_rows), half_rows)
        source = src_ref[source_at, :].astype(F32)
        encoded_ref[chunk, rows, :] = (source + branch).astype(BF16)

        @pl.when((chunk == 0) & (seq == 0) & (core == 0))
        def _():
            encoded_ref[0, :span_rows, :] = jnp.zeros((span_rows, E), BF16)

        share(chunk).start()

    def decode(chunk):
        @pl.when(chunk + 1 < chunks)
        def _():
            load_asks(chunk + 1).start()

        load_asks(chunk).wait()
        share(chunk).wait_recv()

        @pl.loop(0, CHUNK_SPANS // 2)
        def _(pair):
            for row in (2 * pair, 2 * pair + 1):
                decode_span(row, chunk, encoded_ref, asks_ref.at[chunk % 2], blend_ref)

        @pl.when(chunk == 0)
        def _():
            for copy in loads[4:]:
                copy.wait()

        for head in range(blend_ref.shape[0]):
            lanes = slice(head * HD, (head + 1) * HD)
            att_ref[:, lanes] = dot_nn(blend_ref[head], w_value_ref[:, lanes]).astype(BF16)

        for step in range(1, chips + 1):
            slot = step % chips
            give_ref[chunk, slot] = term(far(step), 1 - core).astype(BF16)
            give(chunk, slot).start()
        rows = pl.ds(pl.multiple_of(chunk * CHUNK, CHUNK), CHUNK)
        for step in range(1, chips + 1):
            slot = step % chips
            own = term(far(step), core).astype(BF16).astype(F32)
            give(chunk, slot).wait_recv()
            both = own + take_ref[chunk, slot].astype(F32)
            if slot == 0:
                out_ref[rows, :] = both.astype(BF16)
            else:
                pass_ref[chunk, slot - 1] = both.astype(BF16)
                hand_on(chunk, slot).start()

    @pl.loop(0, chunks + 1)
    def _(step):
        @pl.when(step < chunks)
        def _():
            encode(step)

        @pl.when(step > 0)
        def _():
            decode(step - 1)

    @pl.loop(0, chunks)
    def _(chunk):
        rows = pl.ds(pl.multiple_of(chunk * CHUNK, CHUNK), CHUNK)
        total = out_ref[rows, :].astype(F32)
        for step in range(1, chips):
            hand_on(chunk, step).wait_recv()
            total = total + land_ref[chunk, step - 1].astype(F32)
        out_ref[rows, :] = total.astype(BF16)
        share(chunk).wait_send()
        for slot in range(chips):
            give(chunk, slot).wait_send()
        for step in range(1, chips):
            hand_on(chunk, step).wait_send()


def attend(n_store, src, encq, cond, asks, enc_out, w_value, w_out):
    tokens = cond.shape[1]
    head_width = w_value.shape[1]
    heads = head_width // HD
    width = w_out.shape[1] // n_store
    chips = n_store // CORES
    chunks = tokens // CHUNK
    rows = KNB * NLEN * CHUNK_SPANS
    whole = (src, encq, cond, enc_out, w_value, w_out)
    vmem = pl.BlockSpec(memory_space=pltpu.VMEM)
    return pl.pallas_call(
        functools.partial(attend_kernel, n_store),
        out_shape=jax.ShapeDtypeStruct((tokens, width), BF16),
        in_specs=[pl.BlockSpec(memory_space=pl.ANY)] * 7,
        out_specs=vmem,
        scratch_shapes=[pltpu.VMEM(operand.shape, BF16) for operand in whole]
        + [
            pltpu.VMEM((2, CHUNK_SPANS) + asks.shape[1:], BF16),
            pltpu.VMEM((rows // CORES, E), BF16),
            pltpu.VMEM((chunks, rows, E), BF16),
            pltpu.VMEM((heads, CHUNK, E), BF16),
            pltpu.VMEM((CHUNK, head_width), BF16),
            pltpu.VMEM((chunks, chips, CHUNK, width), BF16),
            pltpu.VMEM((chunks, chips, CHUNK, width), BF16),
            pltpu.VMEM((chunks, chips - 1, CHUNK, width), BF16),
            pltpu.VMEM((chunks, chips - 1, CHUNK, width), BF16),
            pltpu.SemaphoreType.DMA((len(whole),)),
            pltpu.SemaphoreType.DMA((2,)),
            pltpu.SemaphoreType.DMA((chunks,)),
            pltpu.SemaphoreType.DMA((chunks,)),
            pltpu.SemaphoreType.DMA((chunks, chips)),
            pltpu.SemaphoreType.DMA((chunks, chips)),
            pltpu.SemaphoreType.DMA((chunks, chips - 1)),
            pltpu.SemaphoreType.DMA((chunks, chips - 1)),
        ],
        compiler_params=pltpu.CompilerParams(
            collective_id=1, has_side_effects=True, vmem_limit_bytes=62 * 2**20
        ),
        name="attend",
    )(*whole, asks)


def front_kernel(
    outer,
    inner,
    n_store,
    hidden_ref,
    w_query_ref,
    kv_ref,
    nbr_ref,
    ids_ref,
    enc_query_ref,
    w_key_ref,
    asks_out,
    src_out,
    encq_out,
    cond_out,
    hidden_v,
    w_query_v,
    queries_v,
    kv_v,
    acc_v,
    own_v,
    zero_v,
    asks_v,
    table_v,
    src_v,
    encq_v,
    load_sem,
    kv_send,
    kv_recv,
    table_pair,
    table_far,
    table_recv,
    cond_pair,
    cond_far,
    cond_recv,
    tail_sem,
    asks_sem,
):
    seq = lax.axis_index("seq")
    store = lax.axis_index("store")
    n_seq = outer * inner
    a, b = seq // inner, seq % inner
    chips = n_store // CORES
    chip, core = store // CORES, store % CORES
    other = chip * CORES + (1 - core)
    blocks = nbr_ref.shape[0]
    depth = kv_ref.shape[0]
    tokens = hidden_ref.shape[0]
    pieces = tokens // CHUNK
    requests = ids_ref.shape[0]
    has_left, has_right = a > 0, a + 1 < outer
    has_low, has_high = b > 0, b + 1 < inner
    has_next, has_prev = seq + 1 < n_seq, seq > 0

    def far(step):
        return lax.rem(chip + step, chips) * CORES + core

    def far_from(step):
        return lax.rem(chip + chips - step, chips) * CORES + core

    barrier = pltpu.get_barrier_semaphore()

    def greet(seq_at, store_at):
        pl.semaphore_signal(barrier, inc=1, device_id=(seq_at, store_at), device_id_type=MESH)

    greetings = chips
    greet(seq, other)
    for step in range(1, chips):
        greet(seq, far(step))
    for there, target in (
        (has_left, seq - inner),
        (has_right, seq + inner),
        (has_low, seq - 1),
        (has_high, seq + 1),
        (has_next, seq + 1),
        (has_prev, seq - 1),
    ):
        greetings = greetings + there.astype(jnp.int32)

        @pl.when(there)
        def _():
            greet(target, store)

    pl.semaphore_wait(barrier, greetings)

    def load(source, target, at):
        return pltpu.make_async_copy(source, target, load_sem.at[at])

    def kv_copy(slot, way, source=None):
        target = (seq - inner, seq + inner, seq - 1, seq + 1)[way]
        return pltpu.make_async_remote_copy(
            src_ref=kv_v.at[slot] if source is None else source,
            dst_ref=kv_v.at[slot],
            send_sem=kv_send.at[slot, way],
            recv_sem=kv_recv.at[slot],
            device_id=(target, store),
            device_id_type=MESH,
        )

    ways = (has_left, has_right, has_low, has_high)

    def send_kv(slot, which, source=None):
        for way in which:

            @pl.when(ways[way])
            def _():
                kv_copy(slot, way, source).start()

    def table_copy(owner, target, sem, source=None):
        at = table_v.at[pl.ds(owner * blocks, blocks)]
        return pltpu.make_async_remote_copy(
            src_ref=at if source is None else source,
            dst_ref=at,
            send_sem=sem,
            recv_sem=table_recv.at[owner],
            device_id=(seq, target),
            device_id_type=MESH,
        )

    def table_to_pair(owner, source=None):
        return table_copy(owner, other, table_pair.at[owner], source)

    def table_to_far(step):
        return table_copy(store, far(step), table_far.at[step - 1], nbr_ref)

    def cond_copy(piece, owner, target, sem, source=None):
        at = cond_out.at[owner, pl.ds(piece * CHUNK, CHUNK)]
        return pltpu.make_async_remote_copy(
            src_ref=at if source is None else source,
            dst_ref=at,
            send_sem=sem,
            recv_sem=cond_recv.at[piece, owner],
            device_id=(seq, target),
            device_id_type=MESH,
        )

    def cond_to_pair(piece, owner, source=None):
        return cond_copy(piece, owner, other, cond_pair.at[piece, owner], source)

    def cond_to_far(piece, step, source=None):
        return cond_copy(piece, store, far(step), cond_far.at[piece, step - 1], source)

    send_kv(seq, (0, 1, 2, 3), kv_ref)
    for step in range(1, chips):
        table_to_far(step).start()
    table_to_pair(store, nbr_ref).start()
    own_kv = load(kv_ref, kv_v.at[seq], 0)
    own_table = load(nbr_ref, table_v.at[pl.ds(store * blocks, blocks)], 1)
    hidden_load = load(hidden_ref, hidden_v, 2)
    query_load = load(w_query_ref, w_query_v, 3)
    for copy in (own_kv, hidden_load, query_load, own_table):
        copy.start()
    own_kv.wait()
    hidden_load.wait()

    def accumulate(slot, first=False):
        @pl.loop(0, pieces)
        def _(piece):
            rows = pl.ds(pl.multiple_of(piece * CHUNK, CHUNK), CHUNK)
            part = hidden_v[rows, pl.ds(pl.multiple_of(slot * depth, depth), depth)]
            product = dot_nn(part, kv_v[slot])
            if first:
                acc_v[rows, :] = product
            else:
                acc_v[rows, :] += product

    accumulate(seq, first=True)
    query_load.wait()
    query_width = queries_v.shape[1] // 2

    def store_asks(step):
        return pltpu.make_async_copy(
            asks_v.at[step % 2],
            asks_out.at[pl.ds(step * CHUNK_SPANS, CHUNK_SPANS)],
            asks_sem.at[step % 2],
        )

    @pl.loop(0, outer)
    def _(step):
        rows = pl.ds(pl.multiple_of(step * CHUNK, CHUNK), CHUNK)

        @pl.loop(0, 2)
        def _(half):
            lanes = pl.ds(pl.multiple_of(half * query_width, query_width), query_width)
            queries_v[:, lanes] = dot_nn(hidden_v[rows, :], w_query_v[:, lanes]).astype(BF16)

        @pl.when(step >= 2)
        def _():
            store_asks(step - 2).wait()

        for head in range(queries_v.shape[1] // HD):
            lanes = slice(head * HD, (head + 1) * HD)
            asks = dot_nt(queries_v[:, lanes], w_key_ref[:, lanes]).astype(BF16)
            for span in range(CHUNK_SPANS):
                asks_v[step % 2, span, head * CH : (head + 1) * CH, :] = asks[
                    span * CH : (span + 1) * CH
                ]
        store_asks(step).start()

        from_left = (step > 0) & (a >= step)
        from_right = (step > 0) & (a + step < outer)
        left_slot = seq - step * inner
        right_slot = seq + step * inner

        @pl.when(from_left)
        def _():
            kv_copy(left_slot, 1).wait_recv()
            send_kv(left_slot, (1, 2, 3))

        @pl.when(from_right)
        def _():
            kv_copy(right_slot, 0).wait_recv()
            send_kv(right_slot, (0, 2, 3))

        @pl.when(from_left)
        def _():
            accumulate(left_slot)

        @pl.when(from_right)
        def _():
            accumulate(right_slot)

    toward = jnp.where(2 * a < outer, 1, -1)

    @pl.loop(1, inner)
    def _(step):
        @pl.loop(0, outer)
        def _(count):
            line = lax.rem(a + toward * count + outer, outer) * inner + b

            @pl.when(b >= step)
            def _():
                kv_copy(line - step, 3).wait_recv()
                send_kv(line - step, (3,))
                accumulate(line - step)

            @pl.when(b + step < inner)
            def _():
                kv_copy(line + step, 2).wait_recv()
                send_kv(line + step, (2,))
                accumulate(line + step)

    @pl.loop(0, pieces)
    def _(piece):
        rows = pl.ds(pl.multiple_of(piece * CHUNK, CHUNK), CHUNK)
        own_v[rows, :] = acc_v[rows, :].astype(BF16)

    tail = pltpu.make_async_remote_copy(
        src_ref=own_v.at[pl.ds(tokens - CH, CH)],
        dst_ref=cond_out.at[store, pl.ds(0, CH)],
        send_sem=tail_sem.at[0],
        recv_sem=tail_sem.at[1],
        device_id=(seq + 1, store),
        device_id_type=MESH,
    )

    @pl.when(has_next)
    def _():
        tail.start()

    for piece in range(1, pieces):
        source = own_v.at[pl.ds(piece * CHUNK - CH, CHUNK)]
        for step in range(1, chips):
            cond_to_far(piece, step, source).start()
        cond_to_pair(piece, store, source).start()
    body_copy = load(
        own_v.at[pl.ds(0, tokens - CH)], cond_out.at[store, pl.ds(CH, tokens - CH)], 0
    )
    body_copy.start()
    zero_copy = load(zero_v, cond_out.at[store, pl.ds(0, CH)], 2)

    @pl.when(has_prev)
    def _():
        tail.wait_recv()

    @pl.when(jnp.logical_not(has_prev))
    def _():
        zero_v[...] = jnp.zeros_like(zero_v)
        zero_copy.start()
        zero_copy.wait()

    body_copy.wait()
    for step in range(1, chips):
        cond_to_far(0, step).start()
    cond_to_pair(0, store).start()

    own_table.wait()
    for step in range(1, chips):
        table_to_pair(far_from(step)).wait_recv()
        table_to_pair(far_from(step)).start()
    table_to_pair(other).wait_recv()
    for step in range(1, chips):
        mirrored = far_from(step) + 1 - 2 * core
        table_to_pair(mirrored).wait_recv()

    half_spans = CHUNK_SPANS // CORES

    @pl.loop(0, requests // KNB // CORES)
    def _(pair):
        span = (pair // half_spans) * CHUNK_SPANS + core * half_spans + pair % half_spans
        for part in range(KNB):
            request = span * KNB + part
            rows = pl.ds(pl.multiple_of((pair * KNB + part) * NLEN, NLEN), NLEN)
            block = table_v[ids_ref[request]]
            src_v[rows, :] = block
            block = block.astype(F32)
            mean = jnp.mean(block * block, axis=-1, keepdims=True)
            encq_v[rows, :] = (block * lax.rsqrt(mean + EPSILON)).astype(BF16)
        both = pl.ds(pl.multiple_of(pair * KNB * NLEN, KNB * NLEN), KNB * NLEN)
        encq_v[both, :] = dot_nn(encq_v[both, :], enc_query_ref[...]).astype(BF16)

    src_store = load(src_v, src_out, 1)
    encq_store = load(encq_v, encq_out, 2)
    src_store.start()
    encq_store.start()

    order = tuple(range(1, pieces)) + (0,)
    for piece in order:
        for step in range(1, chips):
            cond_to_pair(piece, far_from(step)).wait_recv()
            cond_to_pair(piece, far_from(step)).start()
    for piece in order:
        cond_to_pair(piece, other).wait_recv()
        for step in range(1, chips):
            cond_to_pair(piece, far_from(step) + 1 - 2 * core).wait_recv()

    @pl.when(has_next)
    def _():
        tail.wait_send()

    for piece in order:
        cond_to_pair(piece, store).wait_send()
        for step in range(1, chips):
            cond_to_far(piece, step).wait_send()
            cond_to_pair(piece, far_from(step)).wait_send()
    table_to_pair(store).wait_send()
    for step in range(1, chips):
        table_to_far(step).wait_send()
        table_to_pair(far_from(step)).wait_send()

    def sent(slot, which):
        for way in which:

            @pl.when(ways[way])
            def _():
                kv_copy(slot, way).wait_send()

    @pl.loop(0, outer)
    def _(step):
        @pl.when(step == 0)
        def _():
            sent(seq, (0, 1, 2, 3))

        @pl.when((step > 0) & (a >= step))
        def _():
            sent(seq - step * inner, (1, 2, 3))

        @pl.when((step > 0) & (a + step < outer))
        def _():
            sent(seq + step * inner, (0, 2, 3))

    @pl.loop(1, inner)
    def _(step):
        @pl.loop(0, outer)
        def _(line):
            @pl.when(b >= step)
            def _():
                sent(line * inner + b - step, (3,))

            @pl.when(b + step < inner)
            def _():
                sent(line * inner + b + step, (2,))

    for step in range(max(outer - 2, 0), outer):
        store_asks(step).wait()
    src_store.wait()
    encq_store.wait()


def front(n_seq, n_store, hidden, w_query, own_kv, nbr_table, ids, enc_query, w_key):
    outer = 4
    inner = n_seq // outer
    tokens = hidden.shape[0]
    head_width = w_query.shape[1]
    depth, width = own_kv.shape
    blocks = nbr_table.shape[0] * n_store
    rows = ids.shape[0] * NLEN // CORES
    spans = ids.shape[0] // KNB
    asks = (head_width // HD * CH, E)
    chips = n_store // CORES
    pieces = tokens // CHUNK
    hbm = pl.BlockSpec(memory_space=pl.ANY)
    vmem = pl.BlockSpec(memory_space=pltpu.VMEM)
    smem = pl.BlockSpec(memory_space=pltpu.SMEM)
    dma = pltpu.SemaphoreType.DMA
    return pl.pallas_call(
        functools.partial(front_kernel, outer, inner, n_store),
        out_shape=(
            jax.ShapeDtypeStruct((spans,) + asks, BF16),
            jax.ShapeDtypeStruct((rows, E), BF16),
            jax.ShapeDtypeStruct((rows, E), BF16),
            jax.ShapeDtypeStruct((n_store, tokens, width), BF16),
        ),
        in_specs=[hbm] * 4 + [smem, vmem, vmem],
        out_specs=(hbm,) * 4,
        scratch_shapes=[
            pltpu.VMEM(hidden.shape, BF16),
            pltpu.VMEM(w_query.shape, BF16),
            pltpu.VMEM((CHUNK, head_width), BF16),
            pltpu.VMEM((n_seq, depth, width), BF16),
            pltpu.VMEM((tokens, width), F32),
            pltpu.VMEM((tokens, width), BF16),
            pltpu.VMEM((CH, width), BF16),
            pltpu.VMEM((2, CHUNK_SPANS) + asks, BF16),
            pltpu.VMEM((blocks, NLEN, E), BF16),
            pltpu.VMEM((rows, E), BF16),
            pltpu.VMEM((rows, E), BF16),
            dma((4,)),
            dma((n_seq, 4)),
            dma((n_seq,)),
            dma((n_store,)),
            dma((chips - 1,)),
            dma((n_store,)),
            dma((pieces, n_store)),
            dma((pieces, chips - 1)),
            dma((pieces, n_store)),
            dma((2,)),
            dma((2,)),
        ],
        compiler_params=pltpu.CompilerParams(
            collective_id=2, has_side_effects=True, vmem_limit_bytes=62 * 2**20
        ),
        name="front",
    )(hidden, w_query, own_kv, nbr_table, ids, enc_query, w_key)


def shifted(block, axis, distance):
    devices = range(lax.axis_size(axis))
    route = [(i - distance, i) for i in devices if i - distance in devices]
    return lax.ppermute(block, axis, route)


def body(
    hidden,
    nbr_table,
    nbr_ids,
    w_query,
    w_key,
    w_value,
    w_out,
    enc_query,
    enc_key,
    enc_value,
    enc_out,
):
    n_store = lax.axis_size("store")
    store = lax.axis_index("store")
    own_width = -(-2 * E_TILES // n_store) * LANES
    padding = own_width * n_store - 2 * E
    enc_kv = jnp.concatenate(
        [enc_key, enc_value, jnp.zeros((enc_key.shape[0], padding), BF16)], axis=1
    )
    own_kv = lax.dynamic_slice_in_dim(enc_kv, store * own_width, own_width, axis=1)
    ids = jnp.concatenate([shifted(nbr_ids[-1:], "seq", 1), nbr_ids[:-1]], axis=0)
    asks, src, encq, cond = front(
        lax.axis_size("seq"),
        n_store,
        hidden,
        w_query,
        own_kv,
        nbr_table,
        ids.reshape(-1),
        enc_query,
        w_key,
    )
    return attend(n_store, src, encq, cond, asks, enc_out, w_value, w_out)


def solution(mesh):
    in_specs = (
        P("seq", None),
        P("store", None, None),
        P("seq", None),
        P(None, "store"),
        P(None, "store"),
        P(None, "store"),
        P("store", None),
        P(),
        P("seq", None),
        P("seq", None),
        P(),
    )
    out_specs = P("seq", "store")
    return jax.shard_map(body, mesh=mesh, in_specs=in_specs, out_specs=out_specs, check_vma=False)
```

```python
import functools
import math

import jax
import jax.numpy as jnp
from jax import lax
from jax.experimental import pallas as pl
from jax.experimental.pallas import tpu as pltpu
from jax.sharding import PartitionSpec as P

D = 4096
HD = 128
E = 896
EHD = 64
CH = 64
NLEN = 128
KNB = 2
LANES = 128
E_TILES = E // LANES
EPSILON = 1e-06
CHUNK_SPANS = 4
CHUNK = CHUNK_SPANS * CH
CORES = 2
LOG2E = math.log2(math.e)
MESH = pl.DeviceIdType.MESH
F32 = jnp.float32
BF16 = jnp.bfloat16


def dot_nt(a, b):
    return lax.dot_general(a, b, (((1,), (1,)), ((), ())), preferred_element_type=F32)


def dot_tn(a, b):
    return lax.dot_general(a, b, (((0,), (0,)), ((), ())), preferred_element_type=F32)


def dot_nn(a, b):
    return jnp.dot(a, b, preferred_element_type=F32)


def block_diagonal(rows, heads):
    tiled = jnp.concatenate([rows] * heads, axis=0)
    row_head = lax.broadcasted_iota(jnp.int32, tiled.shape, 0) // EHD
    col_head = lax.broadcasted_iota(jnp.int32, tiled.shape, 1) // EHD
    return jnp.where(row_head == col_head, tiled, jnp.zeros_like(tiled))


def mix_span(span, at_span, row, encq_ref, cond_ref, mixed_ref):
    rows = KNB * NLEN
    at = pl.ds(pl.multiple_of(at_span * rows, rows), rows)
    out_rows = pl.ds(pl.multiple_of(row * rows, rows), rows)
    tokens = pl.ds(pl.multiple_of(span * CH, CH), CH)
    per_device = cond_ref.shape[2] // LANES

    def cond_tile(tile):
        lane = (tile % per_device) * LANES
        return cond_ref[tile // per_device, tokens, lane : lane + LANES]

    for first in range(0, E_TILES, 2):
        tiles = range(first, min(first + 2, E_TILES))
        heads = len(tiles) * LANES // EHD
        lanes = slice(first * LANES, (first + len(tiles)) * LANES)
        keys = jnp.concatenate([cond_tile(t) for t in tiles], axis=1)
        values = jnp.concatenate([cond_tile(E_TILES + t) for t in tiles], axis=1)
        scores = dot_nt(block_diagonal(keys, heads), encq_ref[at, lanes])
        scores = scores.reshape(heads, CH, rows)
        scores = scores - jnp.max(scores, axis=1, keepdims=True)
        exps = jnp.exp2(scores * (LOG2E / math.sqrt(EHD)))
        weights = exps * (1.0 / jnp.sum(exps, axis=1, keepdims=True))
        weights = weights.astype(BF16).reshape(heads * CH, rows)
        mixed_ref[out_rows, lanes] = dot_tn(weights, block_diagonal(values, heads)).astype(BF16)


def decode_span(row, keep_at, encoded_ref, asks_ref, blend_ref):
    rows = pl.ds(pl.multiple_of(row * KNB * NLEN, KNB * NLEN), KNB * NLEN)
    out_rows = pl.ds(pl.multiple_of(row * CH, CH), CH)
    encoded = encoded_ref[keep_at, rows, :]
    scores = dot_nt(asks_ref[row], encoded)
    scores = scores - jnp.max(scores, axis=1, keepdims=True)
    exps = jnp.exp2(scores * (LOG2E / math.sqrt(HD)))
    scale = 1.0 / jnp.sum(exps, axis=1, keepdims=True)
    blend = (dot_nn(exps.astype(BF16), encoded) * scale).astype(BF16)
    for head in range(blend_ref.shape[0]):
        blend_ref[head, out_rows, :] = blend[head * CH : (head + 1) * CH]


def attend_kernel(
    n_store,
    encoded_hbm,
    w_value_hbm,
    w_out_hbm,
    asks_hbm,
    out_ref,
    encoded_ref,
    w_value_ref,
    w_out_ref,
    asks_ref,
    blend_ref,
    att_ref,
    give_ref,
    take_ref,
    pass_ref,
    land_ref,
    load_sem,
    asks_sem,
    encoded_sem,
    give_sem,
    take_sem,
    pass_sem,
    land_sem,
):
    width = out_ref.shape[1]
    chunks = out_ref.shape[0] // CHUNK
    loads = [
        pltpu.make_async_copy(source, target, load_sem.at[at])
        for at, (source, target) in enumerate(
            (
                (w_value_hbm, w_value_ref),
                (w_out_hbm, w_out_ref),
            )
        )
    ]

    def load_asks(chunk):
        return pltpu.make_async_copy(
            asks_hbm.at[pl.ds(chunk * CHUNK_SPANS, CHUNK_SPANS)],
            asks_ref.at[chunk % 2],
            asks_sem.at[chunk % 2],
        )

    def load_encoded(chunk):
        return pltpu.make_async_copy(
            encoded_hbm.at[chunk], encoded_ref.at[chunk], encoded_sem.at[chunk]
        )

    load_encoded(0).start()
    load_asks(0).start()
    for copy in loads:
        copy.start()
    for chunk in range(1, chunks):
        load_encoded(chunk).start()
    seq = lax.axis_index("seq")
    store = lax.axis_index("store")
    chips = n_store // CORES
    chip = store // CORES
    core = store % CORES
    other = chip * CORES + (1 - core)

    def far(step):
        return lax.rem(chip + step, chips)

    barrier = pltpu.get_barrier_semaphore()
    pl.semaphore_signal(barrier, inc=1, device_id=(seq, other), device_id_type=MESH)
    for step in range(1, chips):
        pl.semaphore_signal(
            barrier, inc=1, device_id=(seq, far(step) * CORES + core), device_id_type=MESH
        )
    pl.semaphore_wait(barrier, chips)

    def give(chunk, step):
        return pltpu.make_async_remote_copy(
            src_ref=give_ref.at[chunk, step],
            dst_ref=take_ref.at[chunk, step],
            send_sem=give_sem.at[chunk, step],
            recv_sem=take_sem.at[chunk, step],
            device_id=(seq, other),
            device_id_type=MESH,
        )

    def hand_on(chunk, step):
        return pltpu.make_async_remote_copy(
            src_ref=pass_ref.at[chunk, step - 1],
            dst_ref=land_ref.at[chunk, step - 1],
            send_sem=pass_sem.at[chunk, step - 1],
            recv_sem=land_sem.at[chunk, step - 1],
            device_id=(seq, far(step) * CORES + core),
            device_id_type=MESH,
        )

    def term(chip_at, core_at):
        start = pl.multiple_of((chip_at * CORES + core_at) * width, width)
        return dot_nn(att_ref[...], w_out_ref[:, pl.ds(start, width)])

    def decode(chunk):
        @pl.when(chunk + 1 < chunks)
        def _():
            load_asks(chunk + 1).start()

        load_asks(chunk).wait()
        load_encoded(chunk).wait()

        @pl.loop(0, CHUNK_SPANS // 2)
        def _(pair):
            for row in (2 * pair, 2 * pair + 1):
                decode_span(row, chunk, encoded_ref, asks_ref.at[chunk % 2], blend_ref)

        @pl.when(chunk == 0)
        def _():
            for copy in loads:
                copy.wait()

        for head in range(blend_ref.shape[0]):
            lanes = slice(head * HD, (head + 1) * HD)
            att_ref[:, lanes] = dot_nn(blend_ref[head], w_value_ref[:, lanes]).astype(BF16)

        rows = pl.ds(pl.multiple_of(chunk * CHUNK, CHUNK), CHUNK)
        for step in range(1, chips + 1):
            slot = step % chips
            give_ref[chunk, slot] = term(far(step), 1 - core).astype(BF16)
            give(chunk, slot).start()
            own = term(far(step), core).astype(BF16).astype(F32)
            give(chunk, slot).wait_recv()
            both = (own + take_ref[chunk, slot].astype(F32)).astype(BF16)
            if slot == 0:
                out_ref[rows, :] = both
            else:
                pass_ref[chunk, slot - 1] = both
                hand_on(chunk, slot).start()

    @pl.loop(0, chunks)
    def _(chunk):
        decode(chunk)

    @pl.loop(0, chunks)
    def _(chunk):
        rows = pl.ds(pl.multiple_of(chunk * CHUNK, CHUNK), CHUNK)
        total = out_ref[rows, :].astype(F32)
        for step in range(1, chips):
            hand_on(chunk, step).wait_recv()
            total = total + land_ref[chunk, step - 1].astype(F32)
        out_ref[rows, :] = total.astype(BF16)
        for slot in range(chips):
            give(chunk, slot).wait_send()
        for step in range(1, chips):
            hand_on(chunk, step).wait_send()


def attend(n_store, encoded, asks, w_value, w_out):
    chunks = encoded.shape[0]
    tokens = chunks * CHUNK
    head_width = w_value.shape[1]
    heads = head_width // HD
    width = w_out.shape[1] // n_store
    chips = n_store // CORES
    whole = (encoded, w_value, w_out)
    vmem = pl.BlockSpec(memory_space=pltpu.VMEM)
    return pl.pallas_call(
        functools.partial(attend_kernel, n_store),
        out_shape=jax.ShapeDtypeStruct((tokens, width), BF16),
        in_specs=[pl.BlockSpec(memory_space=pl.ANY)] * 4,
        out_specs=vmem,
        scratch_shapes=[pltpu.VMEM(operand.shape, BF16) for operand in whole]
        + [
            pltpu.VMEM((2, CHUNK_SPANS) + asks.shape[1:], BF16),
            pltpu.VMEM((heads, CHUNK, E), BF16),
            pltpu.VMEM((CHUNK, head_width), BF16),
            pltpu.VMEM((chunks, chips, CHUNK, width), BF16),
            pltpu.VMEM((chunks, chips, CHUNK, width), BF16),
            pltpu.VMEM((chunks, chips - 1, CHUNK, width), BF16),
            pltpu.VMEM((chunks, chips - 1, CHUNK, width), BF16),
            pltpu.SemaphoreType.DMA((len(whole) - 1,)),
            pltpu.SemaphoreType.DMA((2,)),
            pltpu.SemaphoreType.DMA((chunks,)),
            pltpu.SemaphoreType.DMA((chunks, chips)),
            pltpu.SemaphoreType.DMA((chunks, chips)),
            pltpu.SemaphoreType.DMA((chunks, chips - 1)),
            pltpu.SemaphoreType.DMA((chunks, chips - 1)),
        ],
        compiler_params=pltpu.CompilerParams(
            collective_id=1, has_side_effects=True, vmem_limit_bytes=62 * 2**20
        ),
        name="attend",
    )(*whole, asks)


def front_kernel(
    outer,
    inner,
    n_store,
    hidden_ref,
    w_query_ref,
    kv_ref,
    nbr_ref,
    ids_ref,
    enc_query_ref,
    w_key_ref,
    enc_out_ref,
    asks_out,
    encoded_out,
    hidden_v,
    w_query_v,
    queries_v,
    kv_v,
    acc_v,
    own_v,
    zero_v,
    asks_v,
    table_v,
    src_v,
    encq_v,
    cond_v,
    mixed_v,
    load_sem,
    kv_send,
    kv_recv,
    table_pair,
    table_far,
    table_recv,
    cond_pair,
    cond_far,
    cond_recv,
    tail_sem,
    asks_sem,
    share_send,
    share_recv,
    share_local,
):
    seq = lax.axis_index("seq")
    store = lax.axis_index("store")
    n_seq = outer * inner
    a, b = seq // inner, seq % inner
    chips = n_store // CORES
    chip, core = store // CORES, store % CORES
    other = chip * CORES + (1 - core)
    blocks = nbr_ref.shape[0]
    depth = kv_ref.shape[0]
    tokens = hidden_ref.shape[0]
    pieces = tokens // CHUNK
    requests = ids_ref.shape[0]
    has_left, has_right = a > 0, a + 1 < outer
    has_low, has_high = b > 0, b + 1 < inner
    has_next, has_prev = seq + 1 < n_seq, seq > 0

    def far(step):
        return lax.rem(chip + step, chips) * CORES + core

    def far_from(step):
        return lax.rem(chip + chips - step, chips) * CORES + core

    barrier = pltpu.get_barrier_semaphore()

    def greet(seq_at, store_at):
        pl.semaphore_signal(barrier, inc=1, device_id=(seq_at, store_at), device_id_type=MESH)

    greetings = chips
    greet(seq, other)
    for step in range(1, chips):
        greet(seq, far(step))
    for there, target in (
        (has_left, seq - inner),
        (has_right, seq + inner),
        (has_low, seq - 1),
        (has_high, seq + 1),
        (has_next, seq + 1),
        (has_prev, seq - 1),
    ):
        greetings = greetings + there.astype(jnp.int32)

        @pl.when(there)
        def _():
            greet(target, store)

    pl.semaphore_wait(barrier, greetings)

    def load(source, target, at):
        return pltpu.make_async_copy(source, target, load_sem.at[at])

    def kv_copy(slot, way, source=None):
        target = (seq - inner, seq + inner, seq - 1, seq + 1)[way]
        return pltpu.make_async_remote_copy(
            src_ref=kv_v.at[slot] if source is None else source,
            dst_ref=kv_v.at[slot],
            send_sem=kv_send.at[slot, way],
            recv_sem=kv_recv.at[slot],
            device_id=(target, store),
            device_id_type=MESH,
        )

    ways = (has_left, has_right, has_low, has_high)

    def send_kv(slot, which, source=None):
        for way in which:

            @pl.when(ways[way])
            def _():
                kv_copy(slot, way, source).start()

    def table_copy(owner, target, sem, source=None):
        at = table_v.at[pl.ds(owner * blocks, blocks)]
        return pltpu.make_async_remote_copy(
            src_ref=at if source is None else source,
            dst_ref=at,
            send_sem=sem,
            recv_sem=table_recv.at[owner],
            device_id=(seq, target),
            device_id_type=MESH,
        )

    def table_to_pair(owner, source=None):
        return table_copy(owner, other, table_pair.at[owner], source)

    def table_to_far(step):
        return table_copy(store, far(step), table_far.at[step - 1], nbr_ref)

    def cond_copy(piece, owner, target, sem, source=None):
        at = cond_v.at[owner, pl.ds(piece * CHUNK, CHUNK)]
        return pltpu.make_async_remote_copy(
            src_ref=at if source is None else source,
            dst_ref=at,
            send_sem=sem,
            recv_sem=cond_recv.at[piece, owner],
            device_id=(seq, target),
            device_id_type=MESH,
        )

    def cond_to_pair(piece, owner, source=None):
        return cond_copy(piece, owner, other, cond_pair.at[piece, owner], source)

    def cond_to_far(piece, step, source=None):
        return cond_copy(piece, store, far(step), cond_far.at[piece, step - 1], source)

    send_kv(seq, (0, 1, 2, 3), kv_ref)
    for step in range(1, chips):
        table_to_far(step).start()
    table_to_pair(store, nbr_ref).start()
    own_kv = load(kv_ref, kv_v.at[seq], 0)
    own_table = load(nbr_ref, table_v.at[pl.ds(store * blocks, blocks)], 1)
    hidden_load = load(hidden_ref, hidden_v, 2)
    query_load = load(w_query_ref, w_query_v, 3)
    for copy in (own_kv, hidden_load, query_load, own_table):
        copy.start()
    own_kv.wait()
    hidden_load.wait()

    def accumulate(slot, first=False):
        @pl.loop(0, pieces)
        def _(piece):
            rows = pl.ds(pl.multiple_of(piece * CHUNK, CHUNK), CHUNK)
            part = hidden_v[rows, pl.ds(pl.multiple_of(slot * depth, depth), depth)]
            product = dot_nn(part, kv_v[slot])
            if first:
                acc_v[rows, :] = product
            else:
                acc_v[rows, :] += product

    accumulate(seq, first=True)
    query_load.wait()
    query_width = queries_v.shape[1] // 2

    def store_asks(step):
        return pltpu.make_async_copy(
            asks_v.at[step % 2],
            asks_out.at[pl.ds(step * CHUNK_SPANS, CHUNK_SPANS)],
            asks_sem.at[step % 2],
        )

    @pl.loop(0, outer)
    def _(step):
        rows = pl.ds(pl.multiple_of(step * CHUNK, CHUNK), CHUNK)

        @pl.loop(0, 2)
        def _(half):
            lanes = pl.ds(pl.multiple_of(half * query_width, query_width), query_width)
            queries_v[:, lanes] = dot_nn(hidden_v[rows, :], w_query_v[:, lanes]).astype(BF16)

        @pl.when(step >= 2)
        def _():
            store_asks(step - 2).wait()

        for head in range(queries_v.shape[1] // HD):
            lanes = slice(head * HD, (head + 1) * HD)
            asks = dot_nt(queries_v[:, lanes], w_key_ref[:, lanes]).astype(BF16)
            for span in range(CHUNK_SPANS):
                asks_v[step % 2, span, head * CH : (head + 1) * CH, :] = asks[
                    span * CH : (span + 1) * CH
                ]
        store_asks(step).start()

        from_left = (step > 0) & (a >= step)
        from_right = (step > 0) & (a + step < outer)
        left_slot = seq - step * inner
        right_slot = seq + step * inner

        @pl.when(from_left)
        def _():
            kv_copy(left_slot, 1).wait_recv()
            send_kv(left_slot, (1, 2, 3))

        @pl.when(from_right)
        def _():
            kv_copy(right_slot, 0).wait_recv()
            send_kv(right_slot, (0, 2, 3))

        @pl.when(from_left)
        def _():
            accumulate(left_slot)

        @pl.when(from_right)
        def _():
            accumulate(right_slot)

    toward = jnp.where(2 * a < outer, 1, -1)

    @pl.loop(1, inner)
    def _(step):
        @pl.loop(0, outer)
        def _(count):
            line = lax.rem(a + toward * count + outer, outer) * inner + b

            @pl.when(b >= step)
            def _():
                kv_copy(line - step, 3).wait_recv()
                send_kv(line - step, (3,))
                accumulate(line - step)

            @pl.when(b + step < inner)
            def _():
                kv_copy(line + step, 2).wait_recv()
                send_kv(line + step, (2,))
                accumulate(line + step)

    @pl.loop(0, pieces)
    def _(piece):
        rows = pl.ds(pl.multiple_of(piece * CHUNK, CHUNK), CHUNK)
        own_v[rows, :] = acc_v[rows, :].astype(BF16)

    tail = pltpu.make_async_remote_copy(
        src_ref=own_v.at[pl.ds(tokens - CH, CH)],
        dst_ref=cond_v.at[store, pl.ds(0, CH)],
        send_sem=tail_sem.at[0],
        recv_sem=tail_sem.at[1],
        device_id=(seq + 1, store),
        device_id_type=MESH,
    )

    @pl.when(has_next)
    def _():
        tail.start()

    for piece in range(1, pieces):
        source = own_v.at[pl.ds(piece * CHUNK - CH, CHUNK)]
        for step in range(1, chips):
            cond_to_far(piece, step, source).start()
        cond_to_pair(piece, store, source).start()
    body_copy = load(
        own_v.at[pl.ds(0, tokens - CH)], cond_v.at[store, pl.ds(CH, tokens - CH)], 0
    )
    body_copy.start()
    zero_copy = load(zero_v, cond_v.at[store, pl.ds(0, CH)], 2)

    @pl.when(has_prev)
    def _():
        tail.wait_recv()

    @pl.when(jnp.logical_not(has_prev))
    def _():
        zero_v[...] = jnp.zeros_like(zero_v)
        zero_copy.start()
        zero_copy.wait()

    body_copy.wait()
    for step in range(1, chips):
        cond_to_far(0, step).start()
    cond_to_pair(0, store).start()

    own_table.wait()
    for step in range(1, chips):
        table_to_pair(far_from(step)).wait_recv()
        table_to_pair(far_from(step)).start()
    table_to_pair(other).wait_recv()
    for step in range(1, chips):
        mirrored = far_from(step) + 1 - 2 * core
        table_to_pair(mirrored).wait_recv()

    half_spans = CHUNK_SPANS // CORES

    @pl.loop(0, requests // KNB // CORES)
    def _(pair):
        span = (pair // half_spans) * CHUNK_SPANS + core * half_spans + pair % half_spans
        for part in range(KNB):
            request = span * KNB + part
            rows = pl.ds(pl.multiple_of((pair * KNB + part) * NLEN, NLEN), NLEN)
            block = table_v[ids_ref[request]]
            src_v[rows, :] = block
            block = block.astype(F32)
            mean = jnp.mean(block * block, axis=-1, keepdims=True)
            encq_v[rows, :] = (block * lax.rsqrt(mean + EPSILON)).astype(BF16)
        both = pl.ds(pl.multiple_of(pair * KNB * NLEN, KNB * NLEN), KNB * NLEN)
        encq_v[both, :] = dot_nn(encq_v[both, :], enc_query_ref[...]).astype(BF16)

    span_rows = KNB * NLEN
    half_rows = half_spans * span_rows
    own_half = pl.ds(pl.multiple_of(core * half_rows, half_rows), half_rows)

    def rows_of(piece):
        return pl.ds(pl.multiple_of(piece * half_rows, half_rows), half_rows)

    def share(piece):
        return pltpu.make_async_remote_copy(
            src_ref=src_v.at[rows_of(piece)],
            dst_ref=encoded_out.at[piece, own_half],
            send_sem=share_send.at[piece],
            recv_sem=share_recv.at[piece],
            device_id=(seq, other),
            device_id_type=MESH,
        )

    def keep(piece):
        return pltpu.make_async_copy(
            src_v.at[rows_of(piece)], encoded_out.at[piece, own_half], share_local.at[piece]
        )

    @pl.loop(0, pieces)
    def _(count):
        piece = lax.rem(count + 1, pieces)
        for step in range(1, chips):
            cond_to_pair(piece, far_from(step)).wait_recv()
            cond_to_pair(piece, far_from(step)).start()
        cond_to_pair(piece, other).wait_recv()
        for step in range(1, chips):
            cond_to_pair(piece, far_from(step) + 1 - 2 * core).wait_recv()
        for row in range(half_spans):
            span = piece * CHUNK_SPANS + core * half_spans + row
            mix_span(span, piece * half_spans + row, row, encq_v, cond_v, mixed_v)
        branch = dot_nn(mixed_v[...], enc_out_ref[...])
        source = src_v[rows_of(piece), :].astype(F32)
        src_v[rows_of(piece), :] = (source + branch).astype(BF16)

        @pl.when((piece == 0) & (seq == 0) & (core == 0))
        def _():
            src_v[:span_rows, :] = jnp.zeros((span_rows, E), BF16)

        share(piece).start()
        keep(piece).start()

    order = tuple(range(pieces))

    @pl.when(has_next)
    def _():
        tail.wait_send()

    for piece in order:
        cond_to_pair(piece, store).wait_send()
        for step in range(1, chips):
            cond_to_far(piece, step).wait_send()
            cond_to_pair(piece, far_from(step)).wait_send()
    table_to_pair(store).wait_send()
    for step in range(1, chips):
        table_to_far(step).wait_send()
        table_to_pair(far_from(step)).wait_send()

    def sent(slot, which):
        for way in which:

            @pl.when(ways[way])
            def _():
                kv_copy(slot, way).wait_send()

    @pl.loop(0, outer)
    def _(step):
        @pl.when(step == 0)
        def _():
            sent(seq, (0, 1, 2, 3))

        @pl.when((step > 0) & (a >= step))
        def _():
            sent(seq - step * inner, (1, 2, 3))

        @pl.when((step > 0) & (a + step < outer))
        def _():
            sent(seq + step * inner, (0, 2, 3))

    @pl.loop(1, inner)
    def _(step):
        @pl.loop(0, outer)
        def _(line):
            @pl.when(b >= step)
            def _():
                sent(line * inner + b - step, (3,))

            @pl.when(b + step < inner)
            def _():
                sent(line * inner + b + step, (2,))

    for step in range(max(outer - 2, 0), outer):
        store_asks(step).wait()
    for piece in order:
        share(piece).wait_recv()
        share(piece).wait_send()
        keep(piece).wait()


def front(n_seq, n_store, hidden, w_query, own_kv, nbr_table, ids, enc_query, w_key, enc_out):
    outer = 4
    inner = n_seq // outer
    tokens = hidden.shape[0]
    head_width = w_query.shape[1]
    depth, width = own_kv.shape
    blocks = nbr_table.shape[0] * n_store
    rows = ids.shape[0] * NLEN // CORES
    spans = ids.shape[0] // KNB
    asks = (head_width // HD * CH, E)
    chips = n_store // CORES
    pieces = tokens // CHUNK
    hbm = pl.BlockSpec(memory_space=pl.ANY)
    vmem = pl.BlockSpec(memory_space=pltpu.VMEM)
    smem = pl.BlockSpec(memory_space=pltpu.SMEM)
    dma = pltpu.SemaphoreType.DMA
    return pl.pallas_call(
        functools.partial(front_kernel, outer, inner, n_store),
        out_shape=(
            jax.ShapeDtypeStruct((spans,) + asks, BF16),
            jax.ShapeDtypeStruct((pieces, CORES * rows // pieces, E), BF16),
        ),
        in_specs=[hbm] * 4 + [smem, vmem, vmem, vmem],
        out_specs=(hbm,) * 2,
        scratch_shapes=[
            pltpu.VMEM(hidden.shape, BF16),
            pltpu.VMEM(w_query.shape, BF16),
            pltpu.VMEM((CHUNK, head_width), BF16),
            pltpu.VMEM((n_seq, depth, width), BF16),
            pltpu.VMEM((tokens, width), F32),
            pltpu.VMEM((tokens, width), BF16),
            pltpu.VMEM((CH, width), BF16),
            pltpu.VMEM((2, CHUNK_SPANS) + asks, BF16),
            pltpu.VMEM((blocks, NLEN, E), BF16),
            pltpu.VMEM((rows, E), BF16),
            pltpu.VMEM((rows, E), BF16),
            pltpu.VMEM((n_store, tokens, width), BF16),
            pltpu.VMEM((rows // pieces, E), BF16),
            dma((4,)),
            dma((n_seq, 4)),
            dma((n_seq,)),
            dma((n_store,)),
            dma((chips - 1,)),
            dma((n_store,)),
            dma((pieces, n_store)),
            dma((pieces, chips - 1)),
            dma((pieces, n_store)),
            dma((2,)),
            dma((2,)),
            dma((pieces,)),
            dma((pieces,)),
            dma((pieces,)),
        ],
        compiler_params=pltpu.CompilerParams(
            collective_id=2, has_side_effects=True, vmem_limit_bytes=62 * 2**20
        ),
        name="front",
    )(hidden, w_query, own_kv, nbr_table, ids, enc_query, w_key, enc_out)


def shifted(block, axis, distance):
    devices = range(lax.axis_size(axis))
    route = [(i - distance, i) for i in devices if i - distance in devices]
    return lax.ppermute(block, axis, route)


def body(
    hidden,
    nbr_table,
    nbr_ids,
    w_query,
    w_key,
    w_value,
    w_out,
    enc_query,
    enc_key,
    enc_value,
    enc_out,
):
    n_store = lax.axis_size("store")
    store = lax.axis_index("store")
    own_width = -(-2 * E_TILES // n_store) * LANES
    padding = own_width * n_store - 2 * E
    enc_kv = jnp.concatenate(
        [enc_key, enc_value, jnp.zeros((enc_key.shape[0], padding), BF16)], axis=1
    )
    own_kv = lax.dynamic_slice_in_dim(enc_kv, store * own_width, own_width, axis=1)
    ids = jnp.concatenate([shifted(nbr_ids[-1:], "seq", 1), nbr_ids[:-1]], axis=0)
    asks, encoded = front(
        lax.axis_size("seq"),
        n_store,
        hidden,
        w_query,
        own_kv,
        nbr_table,
        ids.reshape(-1),
        enc_query,
        w_key,
        enc_out,
    )
    return attend(n_store, encoded, asks, w_value, w_out)


def solution(mesh):
    in_specs = (
        P("seq", None),
        P("store", None, None),
        P("seq", None),
        P(None, "store"),
        P(None, "store"),
        P(None, "store"),
        P("store", None),
        P(),
        P("seq", None),
        P("seq", None),
        P(),
    )
    out_specs = P("seq", "store")
    return jax.shard_map(body, mesh=mesh, in_specs=in_specs, out_specs=out_specs, check_vma=False)
```

```python
import functools
import math

import jax
import jax.numpy as jnp
from jax import lax
from jax.experimental import pallas as pl
from jax.experimental.pallas import tpu as pltpu
from jax.sharding import PartitionSpec as P

D = 4096
HD = 128
E = 896
EHD = 64
CH = 64
NLEN = 128
KNB = 2
LANES = 128
E_TILES = E // LANES
EPSILON = 1e-06
CHUNK_SPANS = 4
CHUNK = CHUNK_SPANS * CH
CORES = 2
LOG2E = math.log2(math.e)
MESH = pl.DeviceIdType.MESH
F32 = jnp.float32
BF16 = jnp.bfloat16


def dot_nt(a, b):
    return lax.dot_general(a, b, (((1,), (1,)), ((), ())), preferred_element_type=F32)


def dot_tn(a, b):
    return lax.dot_general(a, b, (((0,), (0,)), ((), ())), preferred_element_type=F32)


def dot_nn(a, b):
    return jnp.dot(a, b, preferred_element_type=F32)


def block_diagonal(rows, heads):
    tiled = jnp.concatenate([rows] * heads, axis=0)
    row_head = lax.broadcasted_iota(jnp.int32, tiled.shape, 0) // EHD
    col_head = lax.broadcasted_iota(jnp.int32, tiled.shape, 1) // EHD
    return jnp.where(row_head == col_head, tiled, jnp.zeros_like(tiled))


def mix_span(span, at_span, row, encq_ref, cond_ref, mixed_ref):
    rows = KNB * NLEN
    at = pl.ds(pl.multiple_of(at_span * rows, rows), rows)
    out_rows = pl.ds(pl.multiple_of(row * rows, rows), rows)
    tokens = pl.ds(pl.multiple_of(span * CH, CH), CH)
    per_device = cond_ref.shape[2] // LANES

    def cond_tile(tile):
        lane = (tile % per_device) * LANES
        return cond_ref[tile // per_device, tokens, lane : lane + LANES]

    for first in range(0, E_TILES, 2):
        tiles = range(first, min(first + 2, E_TILES))
        heads = len(tiles) * LANES // EHD
        lanes = slice(first * LANES, (first + len(tiles)) * LANES)
        keys = jnp.concatenate([cond_tile(t) for t in tiles], axis=1)
        values = jnp.concatenate([cond_tile(E_TILES + t) for t in tiles], axis=1)
        scores = dot_nt(block_diagonal(keys, heads), encq_ref[at, lanes])
        scores = scores.reshape(heads, CH, rows)
        scores = scores - jnp.max(scores, axis=1, keepdims=True)
        exps = jnp.exp2(scores * (LOG2E / math.sqrt(EHD)))
        weights = exps * (1.0 / jnp.sum(exps, axis=1, keepdims=True))
        weights = weights.astype(BF16).reshape(heads * CH, rows)
        mixed_ref[out_rows, lanes] = dot_tn(weights, block_diagonal(values, heads)).astype(BF16)


def decode_span(row, keep_at, encoded_ref, asks_ref, blend_ref):
    rows = pl.ds(pl.multiple_of(row * KNB * NLEN, KNB * NLEN), KNB * NLEN)
    out_rows = pl.ds(pl.multiple_of(row * CH, CH), CH)
    encoded = encoded_ref[keep_at, rows, :]
    scores = dot_nt(asks_ref[row], encoded)
    scores = scores - jnp.max(scores, axis=1, keepdims=True)
    exps = jnp.exp2(scores * (LOG2E / math.sqrt(HD)))
    scale = 1.0 / jnp.sum(exps, axis=1, keepdims=True)
    blend = (dot_nn(exps.astype(BF16), encoded) * scale).astype(BF16)
    for head in range(blend_ref.shape[0]):
        blend_ref[head, out_rows, :] = blend[head * CH : (head + 1) * CH]


def attend_kernel(
    n_store,
    src_hbm,
    encq_hbm,
    cond_hbm,
    enc_out_hbm,
    w_value_hbm,
    w_out_hbm,
    asks_hbm,
    out_ref,
    src_ref,
    encq_ref,
    cond_ref,
    enc_out_ref,
    w_value_ref,
    w_out_ref,
    asks_ref,
    mixed_ref,
    encoded_ref,
    blend_ref,
    att_ref,
    give_ref,
    take_ref,
    pass_ref,
    land_ref,
    load_sem,
    asks_sem,
    encoded_send,
    encoded_recv,
    give_sem,
    take_sem,
    pass_sem,
    land_sem,
):
    loads = [
        pltpu.make_async_copy(source, target, load_sem.at[at])
        for at, (source, target) in enumerate(
            (
                (encq_hbm, encq_ref),
                (cond_hbm, cond_ref),
                (src_hbm, src_ref),
                (enc_out_hbm, enc_out_ref),
                (w_value_hbm, w_value_ref),
                (w_out_hbm, w_out_ref),
            )
        )
    ]

    def load_asks(chunk):
        return pltpu.make_async_copy(
            asks_hbm.at[pl.ds(chunk * CHUNK_SPANS, CHUNK_SPANS)],
            asks_ref.at[chunk % 2],
            asks_sem.at[chunk % 2],
        )

    for copy in loads[:4]:
        copy.start()
    load_asks(0).start()
    for copy in loads[4:]:
        copy.start()
    seq = lax.axis_index("seq")
    store = lax.axis_index("store")
    chips = n_store // CORES
    chip = store // CORES
    core = store % CORES
    other = chip * CORES + (1 - core)
    width = out_ref.shape[1]
    chunks = out_ref.shape[0] // CHUNK

    def far(step):
        return lax.rem(chip + step, chips)

    barrier = pltpu.get_barrier_semaphore()
    pl.semaphore_signal(barrier, inc=1, device_id=(seq, other), device_id_type=MESH)
    for step in range(1, chips):
        pl.semaphore_signal(
            barrier, inc=1, device_id=(seq, far(step) * CORES + core), device_id_type=MESH
        )
    pl.semaphore_wait(barrier, chips)

    def give(chunk, step):
        return pltpu.make_async_remote_copy(
            src_ref=give_ref.at[chunk, step],
            dst_ref=take_ref.at[chunk, step],
            send_sem=give_sem.at[chunk, step],
            recv_sem=take_sem.at[chunk, step],
            device_id=(seq, other),
            device_id_type=MESH,
        )

    def hand_on(chunk, step):
        return pltpu.make_async_remote_copy(
            src_ref=pass_ref.at[chunk, step - 1],
            dst_ref=land_ref.at[chunk, step - 1],
            send_sem=pass_sem.at[chunk, step - 1],
            recv_sem=land_sem.at[chunk, step - 1],
            device_id=(seq, far(step) * CORES + core),
            device_id_type=MESH,
        )

    def term(chip_at, core_at):
        start = pl.multiple_of((chip_at * CORES + core_at) * width, width)
        return dot_nn(att_ref[...], w_out_ref[:, pl.ds(start, width)])

    span_rows = KNB * NLEN
    half_spans = CHUNK_SPANS // CORES
    half_rows = half_spans * span_rows

    def share(chunk):
        at = encoded_ref.at[chunk, pl.ds(pl.multiple_of(core * half_rows, half_rows), half_rows)]
        return pltpu.make_async_remote_copy(
            src_ref=at,
            dst_ref=at,
            send_sem=encoded_send.at[chunk],
            recv_sem=encoded_recv.at[chunk],
            device_id=(seq, other),
            device_id_type=MESH,
        )

    def encode(chunk):
        @pl.when(chunk == 0)
        def _():
            for copy in loads[:4]:
                copy.wait()

        for row in range(half_spans):
            span = chunk * CHUNK_SPANS + core * half_spans + row
            mix_span(span, chunk * half_spans + row, row, encq_ref, cond_ref, mixed_ref)
        branch = dot_nn(mixed_ref[...], enc_out_ref[...])
        source_at = pl.ds(pl.multiple_of(chunk * half_rows, half_rows), half_rows)
        rows = pl.ds(pl.multiple_of(core * half_rows, half_rows), half_rows)
        source = src_ref[source_at, :].astype(F32)
        encoded_ref[chunk, rows, :] = (source + branch).astype(BF16)

        @pl.when((chunk == 0) & (seq == 0) & (core == 0))
        def _():
            encoded_ref[0, :span_rows, :] = jnp.zeros((span_rows, E), BF16)

        share(chunk).start()

    def decode(chunk):
        @pl.when(chunk + 1 < chunks)
        def _():
            load_asks(chunk + 1).start()

        load_asks(chunk).wait()
        share(chunk).wait_recv()

        @pl.loop(0, CHUNK_SPANS // 2)
        def _(pair):
            for row in (2 * pair, 2 * pair + 1):
                decode_span(row, chunk, encoded_ref, asks_ref.at[chunk % 2], blend_ref)

        @pl.when(chunk == 0)
        def _():
            for copy in loads[4:]:
                copy.wait()

        for head in range(blend_ref.shape[0]):
            lanes = slice(head * HD, (head + 1) * HD)
            att_ref[:, lanes] = dot_nn(blend_ref[head], w_value_ref[:, lanes]).astype(BF16)

        rows = pl.ds(pl.multiple_of(chunk * CHUNK, CHUNK), CHUNK)
        for step in range(1, chips + 1):
            slot = step % chips
            give_ref[chunk, slot] = term(far(step), 1 - core).astype(BF16)
            give(chunk, slot).start()
            own = term(far(step), core).astype(BF16).astype(F32)
            give(chunk, slot).wait_recv()
            both = (own + take_ref[chunk, slot].astype(F32)).astype(BF16)
            if slot == 0:
                out_ref[rows, :] = both
            else:
                pass_ref[chunk, slot - 1] = both
                hand_on(chunk, slot).start()

    @pl.loop(0, chunks + 1)
    def _(step):
        @pl.when(step < chunks)
        def _():
            encode(step)

        @pl.when(step > 0)
        def _():
            decode(step - 1)

    @pl.loop(0, chunks)
    def _(chunk):
        rows = pl.ds(pl.multiple_of(chunk * CHUNK, CHUNK), CHUNK)
        total = out_ref[rows, :].astype(F32)
        for step in range(1, chips):
            hand_on(chunk, step).wait_recv()
            total = total + land_ref[chunk, step - 1].astype(F32)
        out_ref[rows, :] = total.astype(BF16)
        share(chunk).wait_send()
        for slot in range(chips):
            give(chunk, slot).wait_send()
        for step in range(1, chips):
            hand_on(chunk, step).wait_send()


def attend(n_store, src, encq, cond, asks, enc_out, w_value, w_out):
    tokens = cond.shape[1]
    head_width = w_value.shape[1]
    heads = head_width // HD
    width = w_out.shape[1] // n_store
    chips = n_store // CORES
    chunks = tokens // CHUNK
    rows = KNB * NLEN * CHUNK_SPANS
    whole = (src, encq, cond, enc_out, w_value, w_out)
    vmem = pl.BlockSpec(memory_space=pltpu.VMEM)
    return pl.pallas_call(
        functools.partial(attend_kernel, n_store),
        out_shape=jax.ShapeDtypeStruct((tokens, width), BF16),
        in_specs=[pl.BlockSpec(memory_space=pl.ANY)] * 7,
        out_specs=vmem,
        scratch_shapes=[pltpu.VMEM(operand.shape, BF16) for operand in whole]
        + [
            pltpu.VMEM((2, CHUNK_SPANS) + asks.shape[1:], BF16),
            pltpu.VMEM((rows // CORES, E), BF16),
            pltpu.VMEM((chunks, rows, E), BF16),
            pltpu.VMEM((heads, CHUNK, E), BF16),
            pltpu.VMEM((CHUNK, head_width), BF16),
            pltpu.VMEM((chunks, chips, CHUNK, width), BF16),
            pltpu.VMEM((chunks, chips, CHUNK, width), BF16),
            pltpu.VMEM((chunks, chips - 1, CHUNK, width), BF16),
            pltpu.VMEM((chunks, chips - 1, CHUNK, width), BF16),
            pltpu.SemaphoreType.DMA((len(whole),)),
            pltpu.SemaphoreType.DMA((2,)),
            pltpu.SemaphoreType.DMA((chunks,)),
            pltpu.SemaphoreType.DMA((chunks,)),
            pltpu.SemaphoreType.DMA((chunks, chips)),
            pltpu.SemaphoreType.DMA((chunks, chips)),
            pltpu.SemaphoreType.DMA((chunks, chips - 1)),
            pltpu.SemaphoreType.DMA((chunks, chips - 1)),
        ],
        compiler_params=pltpu.CompilerParams(
            collective_id=1, has_side_effects=True, vmem_limit_bytes=62 * 2**20
        ),
        name="attend",
    )(*whole, asks)


def front_kernel(
    outer,
    inner,
    n_store,
    hidden_ref,
    w_query_ref,
    kv_ref,
    nbr_ref,
    ids_ref,
    enc_query_ref,
    w_key_ref,
    asks_out,
    src_out,
    encq_out,
    cond_out,
    hidden_v,
    w_query_v,
    queries_v,
    kv_v,
    acc_v,
    own_v,
    zero_v,
    asks_v,
    table_v,
    src_v,
    encq_v,
    load_sem,
    kv_send,
    kv_recv,
    table_pair,
    table_far,
    table_recv,
    cond_pair,
    cond_far,
    cond_recv,
    tail_sem,
    asks_sem,
):
    seq = lax.axis_index("seq")
    store = lax.axis_index("store")
    n_seq = outer * inner
    a, b = seq // inner, seq % inner
    chips = n_store // CORES
    chip, core = store // CORES, store % CORES
    other = chip * CORES + (1 - core)
    blocks = nbr_ref.shape[0]
    depth = kv_ref.shape[0]
    tokens = hidden_ref.shape[0]
    pieces = tokens // CHUNK
    requests = ids_ref.shape[0]
    has_left, has_right = a > 0, a + 1 < outer
    has_low, has_high = b > 0, b + 1 < inner
    has_next, has_prev = seq + 1 < n_seq, seq > 0

    def far(step):
        return lax.rem(chip + step, chips) * CORES + core

    def far_from(step):
        return lax.rem(chip + chips - step, chips) * CORES + core

    barrier = pltpu.get_barrier_semaphore()

    def greet(seq_at, store_at):
        pl.semaphore_signal(barrier, inc=1, device_id=(seq_at, store_at), device_id_type=MESH)

    greetings = chips
    greet(seq, other)
    for step in range(1, chips):
        greet(seq, far(step))
    for there, target in (
        (has_left, seq - inner),
        (has_right, seq + inner),
        (has_low, seq - 1),
        (has_high, seq + 1),
        (has_next, seq + 1),
        (has_prev, seq - 1),
    ):
        greetings = greetings + there.astype(jnp.int32)

        @pl.when(there)
        def _():
            greet(target, store)

    pl.semaphore_wait(barrier, greetings)

    def load(source, target, at):
        return pltpu.make_async_copy(source, target, load_sem.at[at])

    def kv_copy(slot, way, source=None):
        target = (seq - inner, seq + inner, seq - 1, seq + 1)[way]
        return pltpu.make_async_remote_copy(
            src_ref=kv_v.at[slot] if source is None else source,
            dst_ref=kv_v.at[slot],
            send_sem=kv_send.at[slot, way],
            recv_sem=kv_recv.at[slot],
            device_id=(target, store),
            device_id_type=MESH,
        )

    ways = (has_left, has_right, has_low, has_high)

    def send_kv(slot, which, source=None):
        for way in which:

            @pl.when(ways[way])
            def _():
                kv_copy(slot, way, source).start()

    def table_copy(owner, target, sem, source=None):
        at = table_v.at[pl.ds(owner * blocks, blocks)]
        return pltpu.make_async_remote_copy(
            src_ref=at if source is None else source,
            dst_ref=at,
            send_sem=sem,
            recv_sem=table_recv.at[owner],
            device_id=(seq, target),
            device_id_type=MESH,
        )

    def table_to_pair(owner, source=None):
        return table_copy(owner, other, table_pair.at[owner], source)

    def table_to_far(step):
        return table_copy(store, far(step), table_far.at[step - 1], nbr_ref)

    def cond_copy(piece, owner, target, sem, source=None):
        at = cond_out.at[owner, pl.ds(piece * CHUNK, CHUNK)]
        return pltpu.make_async_remote_copy(
            src_ref=at if source is None else source,
            dst_ref=at,
            send_sem=sem,
            recv_sem=cond_recv.at[piece, owner],
            device_id=(seq, target),
            device_id_type=MESH,
        )

    def cond_to_pair(piece, owner, source=None):
        return cond_copy(piece, owner, other, cond_pair.at[piece, owner], source)

    def cond_to_far(piece, step, source=None):
        return cond_copy(piece, store, far(step), cond_far.at[piece, step - 1], source)

    send_kv(seq, (0, 1, 2, 3), kv_ref)
    for step in range(1, chips):
        table_to_far(step).start()
    table_to_pair(store, nbr_ref).start()
    own_kv = load(kv_ref, kv_v.at[seq], 0)
    own_table = load(nbr_ref, table_v.at[pl.ds(store * blocks, blocks)], 1)
    hidden_load = load(hidden_ref, hidden_v, 2)
    query_load = load(w_query_ref, w_query_v, 3)
    for copy in (own_kv, hidden_load, query_load, own_table):
        copy.start()
    own_kv.wait()
    hidden_load.wait()

    def accumulate(slot, first=False):
        @pl.loop(0, pieces)
        def _(piece):
            rows = pl.ds(pl.multiple_of(piece * CHUNK, CHUNK), CHUNK)
            part = hidden_v[rows, pl.ds(pl.multiple_of(slot * depth, depth), depth)]
            product = dot_nn(part, kv_v[slot])
            if first:
                acc_v[rows, :] = product
            else:
                acc_v[rows, :] += product

    accumulate(seq, first=True)
    query_load.wait()
    query_width = queries_v.shape[1] // 2

    def store_asks(step):
        return pltpu.make_async_copy(
            asks_v.at[step % 2],
            asks_out.at[pl.ds(step * CHUNK_SPANS, CHUNK_SPANS)],
            asks_sem.at[step % 2],
        )

    @pl.loop(0, outer)
    def _(step):
        rows = pl.ds(pl.multiple_of(step * CHUNK, CHUNK), CHUNK)

        @pl.loop(0, 2)
        def _(half):
            lanes = pl.ds(pl.multiple_of(half * query_width, query_width), query_width)
            queries_v[:, lanes] = dot_nn(hidden_v[rows, :], w_query_v[:, lanes]).astype(BF16)

        @pl.when(step >= 2)
        def _():
            store_asks(step - 2).wait()

        for head in range(queries_v.shape[1] // HD):
            lanes = slice(head * HD, (head + 1) * HD)
            asks = dot_nt(queries_v[:, lanes], w_key_ref[:, lanes]).astype(BF16)
            for span in range(CHUNK_SPANS):
                asks_v[step % 2, span, head * CH : (head + 1) * CH, :] = asks[
                    span * CH : (span + 1) * CH
                ]
        store_asks(step).start()

        from_left = (step > 0) & (a >= step)
        from_right = (step > 0) & (a + step < outer)
        left_slot = seq - step * inner
        right_slot = seq + step * inner

        @pl.when(from_left)
        def _():
            kv_copy(left_slot, 1).wait_recv()
            send_kv(left_slot, (1, 2, 3))

        @pl.when(from_right)
        def _():
            kv_copy(right_slot, 0).wait_recv()
            send_kv(right_slot, (0, 2, 3))

        @pl.when(from_left)
        def _():
            accumulate(left_slot)

        @pl.when(from_right)
        def _():
            accumulate(right_slot)

    toward = jnp.where(2 * a < outer, 1, -1)

    @pl.loop(1, inner)
    def _(step):
        @pl.loop(0, outer)
        def _(count):
            line = lax.rem(a + toward * count + outer, outer) * inner + b

            @pl.when(b >= step)
            def _():
                kv_copy(line - step, 3).wait_recv()
                send_kv(line - step, (3,))
                accumulate(line - step)

            @pl.when(b + step < inner)
            def _():
                kv_copy(line + step, 2).wait_recv()
                send_kv(line + step, (2,))
                accumulate(line + step)

    @pl.loop(0, pieces)
    def _(piece):
        rows = pl.ds(pl.multiple_of(piece * CHUNK, CHUNK), CHUNK)
        own_v[rows, :] = acc_v[rows, :].astype(BF16)

    tail = pltpu.make_async_remote_copy(
        src_ref=own_v.at[pl.ds(tokens - CH, CH)],
        dst_ref=cond_out.at[store, pl.ds(0, CH)],
        send_sem=tail_sem.at[0],
        recv_sem=tail_sem.at[1],
        device_id=(seq + 1, store),
        device_id_type=MESH,
    )

    @pl.when(has_next)
    def _():
        tail.start()

    for piece in range(1, pieces):
        source = own_v.at[pl.ds(piece * CHUNK - CH, CHUNK)]
        for step in range(1, chips):
            cond_to_far(piece, step, source).start()
        cond_to_pair(piece, store, source).start()
    body_copy = load(
        own_v.at[pl.ds(0, tokens - CH)], cond_out.at[store, pl.ds(CH, tokens - CH)], 0
    )
    body_copy.start()
    zero_copy = load(zero_v, cond_out.at[store, pl.ds(0, CH)], 2)

    @pl.when(has_prev)
    def _():
        tail.wait_recv()

    @pl.when(jnp.logical_not(has_prev))
    def _():
        zero_v[...] = jnp.zeros_like(zero_v)
        zero_copy.start()
        zero_copy.wait()

    body_copy.wait()
    for step in range(1, chips):
        cond_to_far(0, step).start()
    cond_to_pair(0, store).start()

    own_table.wait()
    for step in range(1, chips):
        table_to_pair(far_from(step)).wait_recv()
        table_to_pair(far_from(step)).start()
    table_to_pair(other).wait_recv()
    for step in range(1, chips):
        mirrored = far_from(step) + 1 - 2 * core
        table_to_pair(mirrored).wait_recv()

    half_spans = CHUNK_SPANS // CORES

    @pl.loop(0, requests // KNB // CORES)
    def _(pair):
        span = (pair // half_spans) * CHUNK_SPANS + core * half_spans + pair % half_spans
        for part in range(KNB):
            request = span * KNB + part
            rows = pl.ds(pl.multiple_of((pair * KNB + part) * NLEN, NLEN), NLEN)
            block = table_v[ids_ref[request]]
            src_v[rows, :] = block
            block = block.astype(F32)
            mean = jnp.mean(block * block, axis=-1, keepdims=True)
            encq_v[rows, :] = (block * lax.rsqrt(mean + EPSILON)).astype(BF16)
        both = pl.ds(pl.multiple_of(pair * KNB * NLEN, KNB * NLEN), KNB * NLEN)
        encq_v[both, :] = dot_nn(encq_v[both, :], enc_query_ref[...]).astype(BF16)

    src_store = load(src_v, src_out, 1)
    encq_store = load(encq_v, encq_out, 2)
    src_store.start()
    encq_store.start()

    order = tuple(range(1, pieces)) + (0,)
    for piece in order:
        for step in range(1, chips):
            cond_to_pair(piece, far_from(step)).wait_recv()
            cond_to_pair(piece, far_from(step)).start()
    for piece in order:
        cond_to_pair(piece, other).wait_recv()
        for step in range(1, chips):
            cond_to_pair(piece, far_from(step) + 1 - 2 * core).wait_recv()

    @pl.when(has_next)
    def _():
        tail.wait_send()

    for piece in order:
        cond_to_pair(piece, store).wait_send()
        for step in range(1, chips):
            cond_to_far(piece, step).wait_send()
            cond_to_pair(piece, far_from(step)).wait_send()
    table_to_pair(store).wait_send()
    for step in range(1, chips):
        table_to_far(step).wait_send()
        table_to_pair(far_from(step)).wait_send()

    def sent(slot, which):
        for way in which:

            @pl.when(ways[way])
            def _():
                kv_copy(slot, way).wait_send()

    @pl.loop(0, outer)
    def _(step):
        @pl.when(step == 0)
        def _():
            sent(seq, (0, 1, 2, 3))

        @pl.when((step > 0) & (a >= step))
        def _():
            sent(seq - step * inner, (1, 2, 3))

        @pl.when((step > 0) & (a + step < outer))
        def _():
            sent(seq + step * inner, (0, 2, 3))

    @pl.loop(1, inner)
    def _(step):
        @pl.loop(0, outer)
        def _(line):
            @pl.when(b >= step)
            def _():
                sent(line * inner + b - step, (3,))

            @pl.when(b + step < inner)
            def _():
                sent(line * inner + b + step, (2,))

    for step in range(max(outer - 2, 0), outer):
        store_asks(step).wait()
    src_store.wait()
    encq_store.wait()


def front(n_seq, n_store, hidden, w_query, own_kv, nbr_table, ids, enc_query, w_key):
    outer = 4
    inner = n_seq // outer
    tokens = hidden.shape[0]
    head_width = w_query.shape[1]
    depth, width = own_kv.shape
    blocks = nbr_table.shape[0] * n_store
    rows = ids.shape[0] * NLEN // CORES
    spans = ids.shape[0] // KNB
    asks = (head_width // HD * CH, E)
    chips = n_store // CORES
    pieces = tokens // CHUNK
    hbm = pl.BlockSpec(memory_space=pl.ANY)
    vmem = pl.BlockSpec(memory_space=pltpu.VMEM)
    smem = pl.BlockSpec(memory_space=pltpu.SMEM)
    dma = pltpu.SemaphoreType.DMA
    return pl.pallas_call(
        functools.partial(front_kernel, outer, inner, n_store),
        out_shape=(
            jax.ShapeDtypeStruct((spans,) + asks, BF16),
            jax.ShapeDtypeStruct((rows, E), BF16),
            jax.ShapeDtypeStruct((rows, E), BF16),
            jax.ShapeDtypeStruct((n_store, tokens, width), BF16),
        ),
        in_specs=[hbm] * 4 + [smem, vmem, vmem],
        out_specs=(hbm,) * 4,
        scratch_shapes=[
            pltpu.VMEM(hidden.shape, BF16),
            pltpu.VMEM(w_query.shape, BF16),
            pltpu.VMEM((CHUNK, head_width), BF16),
            pltpu.VMEM((n_seq, depth, width), BF16),
            pltpu.VMEM((tokens, width), F32),
            pltpu.VMEM((tokens, width), BF16),
            pltpu.VMEM((CH, width), BF16),
            pltpu.VMEM((2, CHUNK_SPANS) + asks, BF16),
            pltpu.VMEM((blocks, NLEN, E), BF16),
            pltpu.VMEM((rows, E), BF16),
            pltpu.VMEM((rows, E), BF16),
            dma((4,)),
            dma((n_seq, 4)),
            dma((n_seq,)),
            dma((n_store,)),
            dma((chips - 1,)),
            dma((n_store,)),
            dma((pieces, n_store)),
            dma((pieces, chips - 1)),
            dma((pieces, n_store)),
            dma((2,)),
            dma((2,)),
        ],
        compiler_params=pltpu.CompilerParams(
            collective_id=2, has_side_effects=True, vmem_limit_bytes=62 * 2**20
        ),
        name="front",
    )(hidden, w_query, own_kv, nbr_table, ids, enc_query, w_key)


def shifted(block, axis, distance):
    devices = range(lax.axis_size(axis))
    route = [(i - distance, i) for i in devices if i - distance in devices]
    return lax.ppermute(block, axis, route)


def body(
    hidden,
    nbr_table,
    nbr_ids,
    w_query,
    w_key,
    w_value,
    w_out,
    enc_query,
    enc_key,
    enc_value,
    enc_out,
):
    n_store = lax.axis_size("store")
    store = lax.axis_index("store")
    own_width = -(-2 * E_TILES // n_store) * LANES
    padding = own_width * n_store - 2 * E
    enc_kv = jnp.concatenate(
        [enc_key, enc_value, jnp.zeros((enc_key.shape[0], padding), BF16)], axis=1
    )
    own_kv = lax.dynamic_slice_in_dim(enc_kv, store * own_width, own_width, axis=1)
    ids = jnp.concatenate([shifted(nbr_ids[-1:], "seq", 1), nbr_ids[:-1]], axis=0)
    asks, src, encq, cond = front(
        lax.axis_size("seq"),
        n_store,
        hidden,
        w_query,
        own_kv,
        nbr_table,
        ids.reshape(-1),
        enc_query,
        w_key,
    )
    return attend(n_store, src, encq, cond, asks, enc_out, w_value, w_out)


def solution(mesh):
    in_specs = (
        P("seq", None),
        P("store", None, None),
        P("seq", None),
        P(None, "store"),
        P(None, "store"),
        P(None, "store"),
        P("store", None),
        P(),
        P("seq", None),
        P("seq", None),
        P(),
    )
    out_specs = P("seq", "store")
    return jax.shard_map(body, mesh=mesh, in_specs=in_specs, out_specs=out_specs, check_vma=False)
```
